32 devices in a mesh: blk: 8 (over z, y), line: 4 (over x, core).
Axes of the slice: x: 2, y: 2, z: 4, core: 2. Of those that a mesh axis runs over, the one named last changes fastest.
Arguments:
- flow_state: float32 [8, 5, 512, 512], P('blk', None, 'line'), may hold values from -6 to 6
- block_owner: int32 [8], replicated, may hold values from 0 to 7, each once
- link_block: int32 [8, 2], replicated, may hold values from 0 to 7, as said below
- link_side: int32 [8, 2], replicated, may hold values from 0 to 1
- rows_live: int32 [8], replicated, may hold values from 256 to 512, as said below
- x_operator: float32 [512, 1024], replicated, may hold values from -0.25 to 0.25
- ghost_operator: float32 [6, 1024], replicated, may hold values from -1.25 to 1.25
- y_operator: float32 [512, 1024], replicated, may hold values from -0.25 to 0.25
- coefficients: float32 [7], replicated, may hold values from 0.2 to 1
Outputs:
- next_state: float32 [8, 5, 512, 512], P('blk', None, 'line')
The draws below stay inside these ranges and needn't reach their ends.
Inputs may be any that keep to these rules, and one draw needn't show every extreme that they name: link_block and link_side join the blocks' faces in pairs: if face m of block b meets face s of block c, then face s of block c meets face m of block b; no block meets itself. `rows_live`: some block has all 512 lines.
All inputs are finite; a program needn't handle non-finite values.
Results may differ from the reference program's by a relative error of at most 0.0003.
Values sent between devices are 32-bit elements; how exact they have to be, the bound alone decides.
No kernel may reach another device: no remote copies, remote signals or barrier semaphores. Data moves between devices by JAX's collectives and lax.ppermute only.
A program may use at most 64 MiB of HBM per device.

```python
import jax
import jax.numpy as jnp
from jax import lax

XLEN = 512
YLEN = 512
GHOST = 3
NVAR = 5
BLOCKS = 8


def chain_links(key):
    order = jax.random.permutation(jax.random.fold_in(key, 11), BLOCKS).astype(jnp.int32)
    turned = jax.random.randint(jax.random.fold_in(key, 12), (BLOCKS,), 0, 2).astype(jnp.int32)
    after = jnp.roll(order, -1)
    turn_first = turned[order]
    turn_next = turned[after]
    partner = jnp.zeros((BLOCKS, 2), jnp.int32).at[order, 1 - turn_first].set(after).at[after, turn_next].set(order)
    facing = jnp.zeros((BLOCKS, 2), jnp.int32).at[order, 1 - turn_first].set(turn_next).at[after, turn_next].set(1 - turn_first)
    return (partner, facing)


def draw_link_block(key, part):
    return chain_links(key)[0]


def draw_link_side(key, part):
    return chain_links(key)[1]


def draw_rows_live(key, part):
    counts = jax.random.randint(jax.random.fold_in(key, 21), (BLOCKS,), YLEN // 2, YLEN + 1).astype(jnp.int32)
    fullest = jax.random.randint(jax.random.fold_in(key, 22), (), 0, BLOCKS)
    return counts.at[fullest].set(YLEN)


def steps_of(key, dims, shards, low, high):
    level = 1.0
    for axis_at, blocks in shards:
        heights = jax.random.uniform(jax.random.fold_in(jax.random.fold_in(key, 6), axis_at), (blocks,), jnp.float32, low / len(shards), high / len(shards))
        level = level * jnp.repeat(jnp.exp(heights), dims[axis_at] // blocks).reshape((-1,) + (1,) * (len(dims) - 1 - axis_at))
    return level


def noise(own_key, shape, scale, reach, split=(), kind=jnp.bfloat16):
    values = scale * jax.random.normal(own_key, shape, jnp.float32)
    if split:
        values = values * steps_of(own_key, shape, split, -0.22, 0.18)
    return jnp.clip(values, -reach, reach).astype(kind)


def setup_inputs(seed: int = 0) -> dict:
    arg_keys = jax.random.split(jax.random.key(seed), 10)
    flow_state = noise(arg_keys[0], (BLOCKS, NVAR, YLEN, XLEN), 1.0, 6.0, ((0, 8), (2, 4)), jnp.float32)
    block_owner = jax.random.permutation(arg_keys[1], BLOCKS).astype(jnp.int32)
    link_block = draw_link_block(jax.random.fold_in(arg_keys[9], 71), 0)
    link_side = draw_link_side(jax.random.fold_in(arg_keys[9], 71), 0)
    rows_live = draw_rows_live(jax.random.fold_in(arg_keys[9], 71), 0)
    x_operator = noise(arg_keys[5], (XLEN, 2 * XLEN), XLEN ** -0.5, 0.25, (), jnp.float32)
    ghost_operator = noise(arg_keys[6], (2 * GHOST, 2 * XLEN), (8 * GHOST) ** -0.5, 1.25, (), jnp.float32)
    y_operator = noise(arg_keys[7], (YLEN, 2 * YLEN), YLEN ** -0.5, 0.25, (), jnp.float32)
    coefficients = jnp.clip(jax.random.uniform(arg_keys[8], (NVAR + 2,), jnp.float32, 0.2, 1.0), 0.2, 1.0)
    return dict(flow_state=flow_state, block_owner=block_owner, link_block=link_block, link_side=link_side, rows_live=rows_live, x_operator=x_operator, ghost_operator=ghost_operator, y_operator=y_operator, coefficients=coefficients)


highest = lax.Precision.HIGHEST
section_step = 0.3


def reference(flow_state, block_owner, link_block, link_side, rows_live, x_operator, ghost_operator, y_operator, coefficients):
    block_count = block_owner.shape[0]
    slots = jnp.arange(block_count, dtype=jnp.int32)
    block_of = jnp.sum(slots[:, None] * (block_owner[:, None] == slots[None, :]).astype(jnp.int32), axis=0).astype(jnp.int32)
    live_rows = rows_live[block_of]
    y_index = jnp.arange(YLEN, dtype=jnp.int32)
    live_mask = (y_index[None, :] < live_rows[:, None]).astype(jnp.float32)
    masked = flow_state * live_mask[:, None, :, None]
    low_planes = masked[..., :GHOST]
    high_planes = masked[..., XLEN - GHOST:]
    flip_sign = jnp.array([-1.0, 1.0, 1.0, 1.0, 1.0], dtype=jnp.float32)[:, None, None]
    nu_values = coefficients[:NVAR][:, None, None]

    def ghost_side(my_block, my_side):
        partner = link_block[my_block, my_side]
        far_side = link_side[my_block, my_side]
        partner_slot = block_owner[partner]
        chosen = jnp.where(far_side == 0, low_planes[partner_slot], high_planes[partner_slot])
        return jnp.where(far_side == my_side, chosen[..., ::-1] * flip_sign, chosen)

    def advance(slot_index):
        my_block = block_of[slot_index]
        ghost_planes = jnp.concatenate([ghost_side(my_block, 0), ghost_side(my_block, 1)], axis=-1)
        values = masked[slot_index]
        x_parts = jnp.einsum("vyx,xk->vyk", values, x_operator, precision=highest)
        x_parts = x_parts + jnp.einsum("vyg,gk->vyk", ghost_planes, ghost_operator, precision=highest)
        y_parts = jnp.einsum("vyx,yk->vkx", values, y_operator, precision=highest)
        dx_part = x_parts[..., :XLEN]
        dxx_part = x_parts[..., XLEN:]
        dy_part = y_parts[:, :YLEN]
        dyy_part = y_parts[:, YLEN:]
        rhs_terms = -(values[0][None] * dx_part + values[1][None] * dy_part) + nu_values * (dxx_part + dyy_part)
        buoyancy = coefficients[NVAR] * values[3] + coefficients[NVAR + 1] * values[4]
        picker = (jnp.arange(NVAR) == 1).astype(jnp.float32)[:, None, None]
        rhs_terms = rhs_terms + picker * buoyancy[None]
        return (values + section_step * rhs_terms) * live_mask[slot_index][None, :, None]

    return lax.map(advance, slots)
```

```python
import functools

import jax
import jax.numpy as jnp
from jax import lax
from jax.experimental import pallas as pl
from jax.experimental.pallas import tpu as pltpu
from jax.sharding import PartitionSpec as P

GHOST = 3
SECTION_STEP = 0.3
FACE_ROWS = 16
TILE = 256
LANES = 128
FIRST, SECOND = (1, 3), (3, 4)
RAW = tuple(range(FIRST[0], SECOND[1]))
SENT = (0, 4)

SMEM = pltpu.MemorySpace.SMEM
VMEM = pltpu.MemorySpace.VMEM
HBM = pltpu.MemorySpace.HBM


def split_bf16(x):
    hi = x.astype(jnp.bfloat16)
    lo = (x - hi.astype(jnp.float32)).astype(jnp.bfloat16)
    return hi, lo


def dot(a, b):
    return jnp.dot(a, b, preferred_element_type=jnp.float32)


def three_parts(pieces):
    split = [split_bf16(piece) for piece in pieces]
    hi = [s[0] for s in split]
    lo = [s[1] for s in split]
    return jnp.concatenate(hi + hi + lo, axis=0)


def find_block(owner_ref, my_slot):
    return lax.fori_loop(
        0, owner_ref.shape[0], lambda i, found: jnp.where(owner_ref[i] == my_slot, i, found), 0
    )


def faces_kernel(owner_ref, rows_ref, low_ref, high_ref, out_ref):
    nvar, rows, lanes = low_ref.shape[1:]
    live_rows = rows_ref[find_block(owner_ref, lax.axis_index("blk"))]
    y_index = lax.axis_index("line") * rows + lax.broadcasted_iota(jnp.int32, (GHOST, rows), 1)
    live = y_index < live_rows
    for v in range(nvar):
        low = jnp.transpose(low_ref[0, v])[:GHOST]
        high = jnp.transpose(high_ref[0, v])[lanes - GHOST :]
        out_ref[0, 0, GHOST * v : GHOST * (v + 1), :] = jnp.where(live, low, 0.0)
        out_ref[0, 1, GHOST * v : GHOST * (v + 1), :] = jnp.where(live, high, 0.0)
    for m in range(2):
        out_ref[0, m, GHOST * nvar :, :] = jnp.zeros((FACE_ROWS - GHOST * nvar, rows), jnp.float32)


def part_kernel(low, q_ref, out_ref, sem):
    copy = pltpu.make_async_copy(q_ref.at[:, low : low + out_ref.shape[1]], out_ref, sem)
    copy.start()
    copy.wait()


def weights_kernel(
    lines,
    owner_ref,
    rows_ref,
    coef_ref,
    yop_ref,
    wown_ref,
    wnear_ref,
    wdirect_ref,
    wpassed_ref,
    wsend_ref,
    nu_ref,
    columns_ref,
    turned_ref,
    theirs_ref,
    pieces_hi_ref,
    pieces_lo_ref,
    sems,
):
    y_length = yop_ref.shape[0]
    rows = y_length // lines
    line_pos = lax.axis_index("line")
    other = jnp.bitwise_xor(line_pos, 1)
    shifts = range(2, lines, 2)
    targets = [lax.rem(line_pos + s, lines) for s in shifts]

    def column(d, line):
        return pl.ds(pl.multiple_of(d * y_length + (line * rows) // LANES * LANES, LANES), LANES)

    copies = []
    for d in range(2):
        source = yop_ref.at[:, column(d, line_pos)]
        copies.append(pltpu.make_async_copy(source, columns_ref.at[d], sems.at[d]))
    for j, target in enumerate(targets):
        for d in range(2):
            for i, line in enumerate((line_pos, other)):
                source = yop_ref.at[pl.ds(pl.multiple_of(line * rows, 8), rows), column(d, target)]
                goal = theirs_ref.at[j, d, i * rows : (i + 1) * rows]
                copies.append(pltpu.make_async_copy(source, goal, sems.at[len(copies)]))
    for copy in copies:
        copy.start()

    live_rows = rows_ref[find_block(owner_ref, lax.axis_index("blk"))]
    for v in range(nu_ref.shape[0]):
        nu_ref[v] = jnp.full(nu_ref.shape[1:], coef_ref[v], jnp.float32)
    for copy in copies:
        copy.wait()

    shape = (rows, y_length)
    live_in = lax.broadcasted_iota(jnp.int32, shape, 1) < live_rows
    live_out = line_pos * rows + lax.broadcasted_iota(jnp.int32, shape, 0) < live_rows
    offset = pl.multiple_of(lax.rem(line_pos * rows, LANES), 8)
    for d in range(2):
        turned_ref[d] = jnp.transpose(columns_ref[d])
        mine = turned_ref[d, pl.ds(offset, rows), :]
        hi, lo = split_bf16(jnp.where(live_in & live_out, SECTION_STEP * mine, 0.0))
        for p in range(lines):
            pieces_hi_ref[p, d * rows : (d + 1) * rows] = hi[:, p * rows : (p + 1) * rows]
            pieces_lo_ref[p, d * rows : (d + 1) * rows] = lo[:, p * rows : (p + 1) * rows]

    def gather(ref, places):
        hi = [pieces_hi_ref[p] for p in places]
        lo = [pieces_lo_ref[p] for p in places]
        ref[...] = jnp.concatenate(hi + lo + hi, axis=1)

    gather(wown_ref, [line_pos])
    gather(wnear_ref, [other])
    gather(wdirect_ref, [lax.rem(line_pos + lines - s, lines) for s in shifts])
    gather(wpassed_ref, [lax.rem(other + lines - s, lines) for s in shifts])

    shape = (rows, rows)
    ins = [line * rows + lax.broadcasted_iota(jnp.int32, shape, 1) for line in (line_pos, other)]
    live_in = jnp.concatenate(ins, axis=1) < live_rows
    for j, target in enumerate(targets):
        live_out = target * rows + lax.broadcasted_iota(jnp.int32, live_in.shape, 0) < live_rows
        offset = pl.multiple_of(lax.rem(target * rows, LANES), 8)
        for d in range(2):
            turned_ref[d, :, : 2 * rows] = jnp.transpose(theirs_ref[j, d])
            mine = turned_ref[d, pl.ds(offset, rows), : 2 * rows]
            hi, lo = split_bf16(jnp.where(live_in & live_out, SECTION_STEP * mine, 0.0))
            wsend_ref[j, d * rows : (d + 1) * rows] = jnp.concatenate([hi, lo, hi], axis=1)


def own_kernel(
    owner_ref,
    rows_ref,
    coef_ref,
    wown_ref,
    q_ref,
    tile_ref,
    dx_ref,
    dxx_ref,
    out_ref,
    hi_ref,
    lo_ref,
):
    nvar, rows, _ = q_ref.shape[1:]
    live_rows = rows_ref[find_block(owner_ref, lax.axis_index("blk"))]

    @pl.when(pl.program_id(0) == 0)
    def _():
        for v in range(nvar):
            hi, lo = split_bf16(q_ref[0, v])
            hi_ref[v * rows : (v + 1) * rows] = hi
            lo_ref[v * rows : (v + 1) * rows] = lo

    def derivative(op_ref):
        hi, lo = split_bf16(op_ref[...])
        return dot(hi_ref[...], hi) + dot(lo_ref[...], hi) + dot(hi_ref[...], lo)

    dx = derivative(dx_ref)
    dxx = derivative(dxx_ref)
    u, w = tile_ref[0, 0], tile_ref[0, 1]
    live = lax.axis_index("line") * rows + lax.broadcasted_iota(jnp.int32, u.shape, 0) < live_rows
    for v in range(nvar):
        here = slice(v * rows, (v + 1) * rows)
        dy = dot(wown_ref[...], three_parts([tile_ref[0, v]]))
        rhs = coef_ref[v] * dxx[here] - u * dx[here]
        if v == 1:
            rhs = rhs + coef_ref[nvar] * tile_ref[0, 3] + coef_ref[nvar + 1] * tile_ref[0, 4]
        value = jnp.where(live, tile_ref[0, v] + SECTION_STEP * rhs, 0.0)
        out_ref[0, v] = value + coef_ref[v] * dy[rows:] - w * dy[:rows]


def near_kernel(
    face_count,
    owner_ref,
    link_ref,
    side_ref,
    rows_ref,
    gop_ref,
    wnear_ref,
    nu_ref,
    q_ref,
    base_ref,
    near_raw_ref,
    *refs,
):
    near_sent, refs = refs[0], refs[1:]
    faces, (out_ref, left_ref, done_ref, sems) = refs[:face_count], refs[face_count:]
    near = {v: near_sent.at[0, i] for i, v in enumerate(SENT)}
    near.update({v: near_raw_ref.at[0, i] for i, v in enumerate(RAW)})
    nvar, rows, x_length = q_ref.shape[1:]
    my_slot = lax.axis_index("blk")
    my_block = find_block(owner_ref, my_slot)
    sides = [side_ref[m, my_block] for m in range(2)]
    live_rows = rows_ref[my_block]
    y_index = lax.axis_index("line") * rows + lax.broadcasted_iota(jnp.int32, (FACE_ROWS, rows), 1)
    scale = jnp.where(y_index < live_rows, SECTION_STEP, 0.0)

    planes = []
    for m in range(2):
        place = jnp.bitwise_xor(owner_ref[link_ref[m, my_block]], my_slot)
        plane, first = faces[0][0, sides[m]], 1
        for ref in faces[1:]:
            count = ref.shape[0]
            at = jnp.clip(place - first, 0, count - 1)
            plane = jnp.where(place >= first, ref[at, sides[m]], plane)
            first += count
        planes.append(plane * scale)

    def ghost_rows(g):
        parts = []
        for m in range(2):
            straight = g[GHOST * m : GHOST * (m + 1)]
            turned = jnp.concatenate([straight[2:3], straight[1:2], straight[0:1]], axis=0)
            parts.append(jnp.where(sides[m] == m, turned, straight))
        hi, lo = split_bf16(jnp.concatenate(parts, axis=0))
        pad = jnp.zeros((LANES - 6 * GHOST, hi.shape[1]), jnp.float32)
        stacked = [hi.astype(jnp.float32), hi.astype(jnp.float32), lo.astype(jnp.float32)]
        return jnp.concatenate(stacked + [pad], axis=0).astype(jnp.bfloat16)

    operator = ghost_rows(gop_ref[...])
    pad = jnp.zeros((LANES - 6 * GHOST, rows), jnp.float32)
    copies = []
    for v in RAW + SENT:
        parts = []
        for m in range(2):
            part = planes[m][GHOST * v : GHOST * (v + 1)]
            if v == 0:
                part = jnp.where(sides[m] == m, -part, part)
            parts.append(part)
        hi, lo = split_bf16(jnp.concatenate(parts, axis=0))
        stacked = [hi.astype(jnp.float32), lo.astype(jnp.float32), hi.astype(jnp.float32)]
        ghost = jnp.transpose(jnp.concatenate(stacked + [pad], axis=0)).astype(jnp.bfloat16)
        dx = dot(ghost, operator)
        dy = dot(wnear_ref[...], three_parts([near[v][...]]))
        second = nu_ref[v, 0:1] * (dx[:, x_length:] + dy[rows:])
        value = base_ref[0, v] + second - q_ref[0, 0] * dx[:, :x_length] - q_ref[0, 1] * dy[:rows]
        if v in SENT:
            left_ref[0, SENT.index(v)] = value
            continue
        i = RAW.index(v)
        done_ref[i] = value
        copies.append(pltpu.make_async_copy(done_ref.at[i], out_ref.at[0, v], sems.at[i]))
        copies[-1].start()
    for copy in copies:
        copy.wait()


def send_kernel(wsend_ref, nu_ref, q_ref, *refs):
    count = wsend_ref.shape[0]
    near, refs = refs[0], refs[1:]
    far_v, out = refs[:count], refs[count:]
    rows = q_ref.shape[2]
    for j in range(count):
        for i, v in enumerate(SENT):
            dy = dot(wsend_ref[j], three_parts([q_ref[0, v], near[0, i]]))
            out[j][0, i] = nu_ref[v, 0:1] * dy[rows:] - far_v[j][0, 0] * dy[:rows]


def raw_kernel(count, wdirect_ref, wpassed_ref, nu_ref, q_ref, base_ref, *refs):
    out_ref = refs[-1]
    rows = q_ref.shape[2]
    first, second = [(refs[k : k + count], refs[k + count : k + 2 * count]) for k in (0, 2 * count)]
    for (low, high), (direct, passed) in ((FIRST, first), (SECOND, second)):
        for v in range(low, high):
            dy = dot(wdirect_ref[...], three_parts([piece[0, v - low] for piece in direct]))
            dy = dy + dot(wpassed_ref[...], three_parts([piece[0, v - low] for piece in passed]))
            out_ref[0, v] = base_ref[0, v] + nu_ref[v, 0:1] * dy[rows:] - q_ref[0, 1] * dy[:rows]
    for v in SENT:
        out_ref[0, v] = base_ref[0, v]


def last_kernel(left_ref, *refs):
    results, (_, out_ref, done_ref, sems) = refs[:-4], refs[-4:]
    copies = []
    for i, v in enumerate(SENT):
        done_ref[i] = left_ref[0, i] + sum(piece[0, i] for piece in results)
        copies.append(pltpu.make_async_copy(done_ref.at[i], out_ref.at[0, v], sems.at[i]))
        copies[-1].start()
    for copy in copies:
        copy.wait()


def smem():
    return pl.BlockSpec(memory_space=SMEM)


def kept():
    return pl.BlockSpec(memory_space=VMEM)


def held(array):
    return pltpu.with_memory_space_constraint(array, VMEM)


def on_device(
    slots,
    lines,
    flow_state,
    block_owner,
    link_block,
    link_side,
    rows_live,
    x_operator,
    ghost_operator,
    y_operator,
    coefficients,
):
    _, nvar, rows, x_length = flow_state.shape
    y_length = lines * rows
    limit = pltpu.CompilerParams(vmem_limit_bytes=16 * 1024 * 1024)
    small = pl.CostEstimate(flops=1, bytes_accessed=1, transcendentals=0)
    state_shape = jax.ShapeDtypeStruct(flow_state.shape, jnp.float32)
    sibling = [(i, i ^ 1) for i in range(lines)]
    shifts = range(2, lines, 2)

    def across(array):
        return [lax.ppermute(array, "line", [(i, (i + s) % lines) for i in range(lines)]) for s in shifts]

    low, high = FIRST
    part = pl.pallas_call(
        functools.partial(part_kernel, low),
        in_specs=[pl.BlockSpec(memory_space=pl.ANY)],
        out_specs=pl.BlockSpec(memory_space=VMEM),
        out_shape=jax.ShapeDtypeStruct((1, high - low, rows, x_length), jnp.float32),
        scratch_shapes=[pltpu.SemaphoreType.DMA],
        compiler_params=limit,
        cost_estimate=small,
        name="part",
    )(pltpu.with_memory_space_constraint(flow_state, HBM))
    part, flow_state = lax.optimization_barrier((part, flow_state))
    direct_first = across(part)
    second = flow_state[:, SECOND[0] : SECOND[1]]
    direct_second = across(second)
    near_sent = lax.ppermute(
        jnp.concatenate([flow_state[:, v : v + 1] for v in SENT], axis=1), "line", sibling
    )

    last = x_length // LANES - 1
    faces = pl.pallas_call(
        faces_kernel,
        grid=(1,),
        in_specs=[
            smem(),
            smem(),
            pl.BlockSpec((1, nvar, rows, LANES), lambda i: (0, 0, 0, 0)),
            pl.BlockSpec((1, nvar, rows, LANES), lambda i: (0, 0, 0, last)),
        ],
        out_specs=pl.BlockSpec((1, 2, FACE_ROWS, rows), lambda i: (0, 0, 0, 0)),
        out_shape=jax.ShapeDtypeStruct((1, 2, FACE_ROWS, rows), jnp.float32),
        compiler_params=limit,
        cost_estimate=small,
        name="faces",
    )(block_owner, rows_live, flow_state, flow_state)

    w_near = jax.ShapeDtypeStruct((2 * rows, 3 * rows), jnp.bfloat16)
    w_far = jax.ShapeDtypeStruct((2 * rows, 3 * len(shifts) * rows), jnp.bfloat16)
    w_send = jax.ShapeDtypeStruct((len(shifts), 2 * rows, 6 * rows), jnp.bfloat16)
    nu = jax.ShapeDtypeStruct((nvar, 8, x_length), jnp.float32)
    w_own, w_near, w_direct, w_passed, w_send, nu = pl.pallas_call(
        functools.partial(weights_kernel, lines),
        in_specs=[smem()] * 3 + [pl.BlockSpec(memory_space=pl.ANY)],
        out_specs=[kept()] * 6,
        out_shape=[w_near, w_near, w_far, w_far, w_send, nu],
        scratch_shapes=[
            pltpu.VMEM((2, y_length, LANES), jnp.float32),
            pltpu.VMEM((2, LANES, y_length), jnp.float32),
            pltpu.VMEM((len(shifts), 2, 2 * rows, LANES), jnp.float32),
            pltpu.VMEM((lines, 2 * rows, rows), jnp.bfloat16),
            pltpu.VMEM((lines, 2 * rows, rows), jnp.bfloat16),
            pltpu.SemaphoreType.DMA((2 + 4 * len(shifts),)),
        ],
        compiler_params=limit,
        cost_estimate=small,
        name="weights",
    )(block_owner, rows_live, coefficients, pltpu.with_memory_space_constraint(y_operator, HBM))

    tiles = x_length // TILE
    def own_terms(w_own):
        return pl.pallas_call(
            own_kernel,
            grid=(tiles,),
            in_specs=[smem()] * 3
            + [
                pl.BlockSpec(w_own.shape, lambda n: (0, 0)),
                pl.BlockSpec((1, nvar, rows, x_length), lambda n: (0, 0, 0, 0)),
                pl.BlockSpec((1, nvar, rows, TILE), lambda n: (0, 0, 0, n)),
                pl.BlockSpec((x_length, TILE), lambda n: (0, n)),
                pl.BlockSpec((x_length, TILE), lambda n: (0, n + tiles)),
            ],
            out_specs=pl.BlockSpec((1, nvar, rows, TILE), lambda n: (0, 0, 0, n)),
            out_shape=state_shape,
            scratch_shapes=[
                pltpu.VMEM((nvar * rows, x_length), jnp.bfloat16),
                pltpu.VMEM((nvar * rows, x_length), jnp.bfloat16),
            ],
            compiler_params=limit,
            cost_estimate=small,
            name="own_terms",
        )(
            block_owner,
            rows_live,
            coefficients,
            w_own,
            flow_state,
            flow_state,
            *[pltpu.with_memory_space_constraint(x_operator, HBM)] * 2,
        )

    far_v = [direct_first[shifts.index(lines - s)] for s in shifts]
    sent = jax.ShapeDtypeStruct((1, len(SENT), rows, x_length), jnp.float32)
    send = pl.pallas_call(
        send_kernel,
        in_specs=[kept()] * (4 + len(shifts)),
        out_specs=[kept()] * len(shifts),
        out_shape=[sent] * len(shifts),
        compiler_params=limit,
        cost_estimate=small,
        name="send_terms",
    )
    arrived = [faces]
    held_faces, step = faces, 1
    while step < slots:
        there = lax.ppermute(held_faces, "blk", [(i, i ^ step) for i in range(slots)])
        if step == 1:
            there, w_own, own = lax.optimization_barrier((there, w_own, flow_state))
            near_raw = lax.ppermute(own[:, RAW[0] : RAW[-1] + 1], "line", sibling)
        elif step == 2:
            state = own_terms(w_own)
            w_send, *_ = lax.optimization_barrier((w_send, state, there))
            results = send(*map(held, (w_send, nu, flow_state, near_sent, *far_v)))
            direct_first, *_ = lax.optimization_barrier((direct_first, *results))
            direct_second, *_ = lax.optimization_barrier((direct_second, *results))
        arrived.append(there)
        step *= 2
        if step < slots:
            held_faces = jnp.concatenate([held_faces, there], axis=0)

    results = [
        lax.ppermute(result, "line", [(i, (i + s) % lines) for i in range(lines)])
        for s, result in zip(shifts, results)
    ]

    passed_first = [lax.ppermute(piece, "line", sibling) for piece in direct_first]
    passed_second = [lax.ppermute(piece, "line", sibling) for piece in direct_second]
    pieces = [*direct_first, *passed_first, *direct_second, *passed_second]
    state = pl.pallas_call(
        functools.partial(raw_kernel, len(shifts)),
        in_specs=[kept()] * (5 + len(pieces)),
        out_specs=kept(),
        out_shape=state_shape,
        compiler_params=limit,
        cost_estimate=small,
        name="raw_terms",
    )(*map(held, (w_direct, w_passed, nu, flow_state, state, *pieces)))

    anywhere = pl.BlockSpec(memory_space=pl.ANY)
    result, left = pl.pallas_call(
        functools.partial(near_kernel, len(arrived)),
        in_specs=[smem()] * 4 + [kept()] * (7 + len(arrived)),
        out_specs=[anywhere, kept()],
        out_shape=[state_shape, sent],
        scratch_shapes=[
            pltpu.VMEM((len(RAW), rows, x_length), jnp.float32),
            pltpu.SemaphoreType.DMA((len(RAW),)),
        ],
        compiler_params=limit,
        cost_estimate=small,
        name="near_terms",
    )(
        block_owner,
        link_block.T,
        link_side.T,
        rows_live,
        *map(held, (ghost_operator, w_near, nu, flow_state, state, near_raw, near_sent, *arrived)),
    )

    operands = [*map(held, (left, *results))]
    return pl.pallas_call(
        last_kernel,
        in_specs=[kept()] * len(operands) + [anywhere],
        out_specs=anywhere,
        out_shape=state_shape,
        input_output_aliases={len(operands): 0},
        scratch_shapes=[pltpu.VMEM(sent.shape[1:], jnp.float32), pltpu.SemaphoreType.DMA((len(SENT),))],
        compiler_params=limit,
        cost_estimate=small,
        name="last_terms",
    )(*operands, result)


def solution(mesh):
    return jax.shard_map(
        functools.partial(on_device, mesh.shape["blk"], mesh.shape["line"]),
        mesh=mesh,
        in_specs=(P("blk", None, "line", None), P(), P(), P(), P(), P(), P(), P(), P()),
        out_specs=P("blk", None, "line", None),
        check_vma=False,
    )
```

```python
import functools

import jax
import jax.numpy as jnp
from jax import lax
from jax.experimental import pallas as pl
from jax.experimental.pallas import tpu as pltpu
from jax.sharding import PartitionSpec as P

GHOST = 3
SECTION_STEP = 0.3
FACE_ROWS = 16
TILE = 256
LANES = 128
PIECES = 4
FIRST, SECOND = (1, 3), (3, 4)
RAW = tuple(range(FIRST[0], SECOND[1]))
SENT = (0, 4)

SMEM = pltpu.MemorySpace.SMEM
VMEM = pltpu.MemorySpace.VMEM
HBM = pltpu.MemorySpace.HBM


def split_bf16(x):
    hi = x.astype(jnp.bfloat16)
    lo = (x - hi.astype(jnp.float32)).astype(jnp.bfloat16)
    return hi, lo


def dot(a, b):
    return jnp.dot(a, b, preferred_element_type=jnp.float32)


def three_parts(pieces):
    split = [split_bf16(piece) for piece in pieces]
    hi = [s[0] for s in split]
    lo = [s[1] for s in split]
    return jnp.concatenate(hi + hi + lo, axis=0)


def find_block(owner_ref, my_slot):
    return lax.fori_loop(
        0, owner_ref.shape[0], lambda i, found: jnp.where(owner_ref[i] == my_slot, i, found), 0
    )


def faces_kernel(owner_ref, rows_ref, low_ref, high_ref, out_ref):
    nvar, rows, lanes = low_ref.shape[1:]
    live_rows = rows_ref[find_block(owner_ref, lax.axis_index("blk"))]
    y_index = lax.axis_index("line") * rows + lax.broadcasted_iota(jnp.int32, (GHOST, rows), 1)
    live = y_index < live_rows
    for v in range(nvar):
        low = jnp.transpose(low_ref[0, v])[:GHOST]
        high = jnp.transpose(high_ref[0, v])[lanes - GHOST :]
        out_ref[0, 0, GHOST * v : GHOST * (v + 1), :] = jnp.where(live, low, 0.0)
        out_ref[0, 1, GHOST * v : GHOST * (v + 1), :] = jnp.where(live, high, 0.0)
    for m in range(2):
        out_ref[0, m, GHOST * nvar :, :] = jnp.zeros((FACE_ROWS - GHOST * nvar, rows), jnp.float32)


def part_kernel(low, q_ref, out_ref, sems):
    size = out_ref.shape[2] // PIECES
    copies = []
    for i in range(out_ref.shape[1]):
        for j in range(PIECES):
            here = pl.ds(j * size, size)
            source, goal = q_ref.at[0, low + i, here], out_ref.at[0, i, here]
            copies.append(pltpu.make_async_copy(source, goal, sems.at[len(copies)]))
    for copy in copies:
        copy.start()
    for copy in copies:
        copy.wait()


def weights_kernel(
    lines,
    owner_ref,
    rows_ref,
    coef_ref,
    yop_ref,
    wown_ref,
    wnear_ref,
    wdirect_ref,
    wpassed_ref,
    wsend_ref,
    nu_ref,
    columns_ref,
    turned_ref,
    theirs_ref,
    pieces_hi_ref,
    pieces_lo_ref,
    sems,
):
    y_length = yop_ref.shape[0]
    rows = y_length // lines
    line_pos = lax.axis_index("line")
    other = jnp.bitwise_xor(line_pos, 1)
    shifts = range(2, lines, 2)
    targets = [lax.rem(line_pos + s, lines) for s in shifts]

    def column(d, line):
        return pl.ds(pl.multiple_of(d * y_length + (line * rows) // LANES * LANES, LANES), LANES)

    copies = []
    for d in range(2):
        source = yop_ref.at[:, column(d, line_pos)]
        copies.append(pltpu.make_async_copy(source, columns_ref.at[d], sems.at[d]))
    for j, target in enumerate(targets):
        for d in range(2):
            for i, line in enumerate((line_pos, other)):
                source = yop_ref.at[pl.ds(pl.multiple_of(line * rows, 8), rows), column(d, target)]
                goal = theirs_ref.at[j, d, i * rows : (i + 1) * rows]
                copies.append(pltpu.make_async_copy(source, goal, sems.at[len(copies)]))
    for copy in copies:
        copy.start()

    live_rows = rows_ref[find_block(owner_ref, lax.axis_index("blk"))]
    for v in range(nu_ref.shape[0]):
        nu_ref[v] = jnp.full(nu_ref.shape[1:], coef_ref[v], jnp.float32)
    for copy in copies:
        copy.wait()

    shape = (rows, y_length)
    live_in = lax.broadcasted_iota(jnp.int32, shape, 1) < live_rows
    live_out = line_pos * rows + lax.broadcasted_iota(jnp.int32, shape, 0) < live_rows
    offset = pl.multiple_of(lax.rem(line_pos * rows, LANES), 8)
    for d in range(2):
        turned_ref[d] = jnp.transpose(columns_ref[d])
        mine = turned_ref[d, pl.ds(offset, rows), :]
        hi, lo = split_bf16(jnp.where(live_in & live_out, SECTION_STEP * mine, 0.0))
        for p in range(lines):
            pieces_hi_ref[p, d * rows : (d + 1) * rows] = hi[:, p * rows : (p + 1) * rows]
            pieces_lo_ref[p, d * rows : (d + 1) * rows] = lo[:, p * rows : (p + 1) * rows]

    def gather(ref, places):
        hi = [pieces_hi_ref[p] for p in places]
        lo = [pieces_lo_ref[p] for p in places]
        ref[...] = jnp.concatenate(hi + lo + hi, axis=1)

    gather(wown_ref, [line_pos])
    gather(wnear_ref, [other])
    gather(wdirect_ref, [lax.rem(line_pos + lines - s, lines) for s in shifts])
    gather(wpassed_ref, [lax.rem(other + lines - s, lines) for s in shifts])

    shape = (rows, rows)
    ins = [line * rows + lax.broadcasted_iota(jnp.int32, shape, 1) for line in (line_pos, other)]
    live_in = jnp.concatenate(ins, axis=1) < live_rows
    for j, target in enumerate(targets):
        live_out = target * rows + lax.broadcasted_iota(jnp.int32, live_in.shape, 0) < live_rows
        offset = pl.multiple_of(lax.rem(target * rows, LANES), 8)
        for d in range(2):
            turned_ref[d, :, : 2 * rows] = jnp.transpose(theirs_ref[j, d])
            mine = turned_ref[d, pl.ds(offset, rows), : 2 * rows]
            hi, lo = split_bf16(jnp.where(live_in & live_out, SECTION_STEP * mine, 0.0))
            wsend_ref[j, d * rows : (d + 1) * rows] = jnp.concatenate([hi, lo, hi], axis=1)


def own_kernel(
    owner_ref,
    rows_ref,
    coef_ref,
    wown_ref,
    q_ref,
    tile_ref,
    dx_ref,
    dxx_ref,
    out_ref,
    hi_ref,
    lo_ref,
):
    nvar, rows, _ = q_ref.shape[1:]
    live_rows = rows_ref[find_block(owner_ref, lax.axis_index("blk"))]

    @pl.when(pl.program_id(0) == 0)
    def _():
        for v in range(nvar):
            hi, lo = split_bf16(q_ref[0, v])
            hi_ref[v * rows : (v + 1) * rows] = hi
            lo_ref[v * rows : (v + 1) * rows] = lo

    def derivative(op_ref):
        hi, lo = split_bf16(op_ref[...])
        return dot(hi_ref[...], hi) + dot(lo_ref[...], hi) + dot(hi_ref[...], lo)

    dx = derivative(dx_ref)
    dxx = derivative(dxx_ref)
    u, w = tile_ref[0, 0], tile_ref[0, 1]
    live = lax.axis_index("line") * rows + lax.broadcasted_iota(jnp.int32, u.shape, 0) < live_rows
    for v in range(nvar):
        here = slice(v * rows, (v + 1) * rows)
        dy = dot(wown_ref[...], three_parts([tile_ref[0, v]]))
        rhs = coef_ref[v] * dxx[here] - u * dx[here]
        if v == 1:
            rhs = rhs + coef_ref[nvar] * tile_ref[0, 3] + coef_ref[nvar + 1] * tile_ref[0, 4]
        value = jnp.where(live, tile_ref[0, v] + SECTION_STEP * rhs, 0.0)
        out_ref[0, v] = value + coef_ref[v] * dy[rows:] - w * dy[:rows]


def near_kernel(
    face_count,
    owner_ref,
    link_ref,
    side_ref,
    rows_ref,
    gop_ref,
    wnear_ref,
    nu_ref,
    q_ref,
    base_ref,
    near_raw_ref,
    *refs,
):
    near_sent, refs = refs[0], refs[1:]
    faces, (out_ref, left_ref, done_ref, sems) = refs[:face_count], refs[face_count:]
    near = {v: near_sent.at[0, i] for i, v in enumerate(SENT)}
    near.update({v: near_raw_ref.at[0, i] for i, v in enumerate(RAW)})
    nvar, rows, x_length = q_ref.shape[1:]
    my_slot = lax.axis_index("blk")
    my_block = find_block(owner_ref, my_slot)
    sides = [side_ref[m, my_block] for m in range(2)]
    live_rows = rows_ref[my_block]
    y_index = lax.axis_index("line") * rows + lax.broadcasted_iota(jnp.int32, (FACE_ROWS, rows), 1)
    scale = jnp.where(y_index < live_rows, SECTION_STEP, 0.0)

    planes = []
    for m in range(2):
        place = jnp.bitwise_xor(owner_ref[link_ref[m, my_block]], my_slot)
        plane, first = faces[0][0, sides[m]], 1
        for ref in faces[1:]:
            count = ref.shape[0]
            at = jnp.clip(place - first, 0, count - 1)
            plane = jnp.where(place >= first, ref[at, sides[m]], plane)
            first += count
        planes.append(plane * scale)

    def ghost_rows(g):
        parts = []
        for m in range(2):
            straight = g[GHOST * m : GHOST * (m + 1)]
            turned = jnp.concatenate([straight[2:3], straight[1:2], straight[0:1]], axis=0)
            parts.append(jnp.where(sides[m] == m, turned, straight))
        hi, lo = split_bf16(jnp.concatenate(parts, axis=0))
        pad = jnp.zeros((LANES - 6 * GHOST, hi.shape[1]), jnp.float32)
        stacked = [hi.astype(jnp.float32), hi.astype(jnp.float32), lo.astype(jnp.float32)]
        return jnp.concatenate(stacked + [pad], axis=0).astype(jnp.bfloat16)

    operator = ghost_rows(gop_ref[...])
    pad = jnp.zeros((LANES - 6 * GHOST, rows), jnp.float32)
    copies = []
    for v in RAW + SENT:
        parts = []
        for m in range(2):
            part = planes[m][GHOST * v : GHOST * (v + 1)]
            if v == 0:
                part = jnp.where(sides[m] == m, -part, part)
            parts.append(part)
        hi, lo = split_bf16(jnp.concatenate(parts, axis=0))
        stacked = [hi.astype(jnp.float32), lo.astype(jnp.float32), hi.astype(jnp.float32)]
        ghost = jnp.transpose(jnp.concatenate(stacked + [pad], axis=0)).astype(jnp.bfloat16)
        dx = dot(ghost, operator)
        dy = dot(wnear_ref[...], three_parts([near[v][...]]))
        second = nu_ref[v, 0:1] * (dx[:, x_length:] + dy[rows:])
        value = base_ref[0, v] + second - q_ref[0, 0] * dx[:, :x_length] - q_ref[0, 1] * dy[:rows]
        if v in SENT:
            left_ref[0, SENT.index(v)] = value
            continue
        i = RAW.index(v)
        done_ref[i] = value
        copies.append(pltpu.make_async_copy(done_ref.at[i], out_ref.at[0, v], sems.at[i]))
        copies[-1].start()
    for copy in copies:
        copy.wait()


def send_kernel(wsend_ref, nu_ref, q_ref, *refs):
    count = wsend_ref.shape[0]
    near, refs = refs[0], refs[1:]
    far_v, out = refs[:count], refs[count:]
    rows = q_ref.shape[2]
    for j in range(count):
        for i, v in enumerate(SENT):
            dy = dot(wsend_ref[j], three_parts([q_ref[0, v], near[0, i]]))
            out[j][0, i] = nu_ref[v, 0:1] * dy[rows:] - far_v[j][0, 0] * dy[:rows]


def raw_kernel(count, wdirect_ref, wpassed_ref, nu_ref, q_ref, base_ref, *refs):
    out_ref = refs[-1]
    rows = q_ref.shape[2]
    first, second = [(refs[k : k + count], refs[k + count : k + 2 * count]) for k in (0, 2 * count)]
    for (low, high), (direct, passed) in ((FIRST, first), (SECOND, second)):
        for v in range(low, high):
            dy = dot(wdirect_ref[...], three_parts([piece[0, v - low] for piece in direct]))
            dy = dy + dot(wpassed_ref[...], three_parts([piece[0, v - low] for piece in passed]))
            out_ref[0, v] = base_ref[0, v] + nu_ref[v, 0:1] * dy[rows:] - q_ref[0, 1] * dy[:rows]
    for v in SENT:
        out_ref[0, v] = base_ref[0, v]


def last_kernel(left_ref, *refs):
    results, (_, out_ref, done_ref, sems) = refs[:-4], refs[-4:]
    copies = []
    size = left_ref.shape[2] // PIECES
    for i, v in enumerate(SENT):
        for j in range(PIECES):
            here = pl.ds(j * size, size)
            done_ref[i, here] = left_ref[0, i, here] + sum(piece[0, i, here] for piece in results)
            source, goal = done_ref.at[i, here], out_ref.at[0, v, here]
            copies.append(pltpu.make_async_copy(source, goal, sems.at[len(copies)]))
            copies[-1].start()
    for copy in copies:
        copy.wait()


def smem():
    return pl.BlockSpec(memory_space=SMEM)


def kept():
    return pl.BlockSpec(memory_space=VMEM)


def held(array):
    return pltpu.with_memory_space_constraint(array, VMEM)


def on_device(
    slots,
    lines,
    flow_state,
    block_owner,
    link_block,
    link_side,
    rows_live,
    x_operator,
    ghost_operator,
    y_operator,
    coefficients,
):
    _, nvar, rows, x_length = flow_state.shape
    y_length = lines * rows
    limit = pltpu.CompilerParams(vmem_limit_bytes=16 * 1024 * 1024)
    small = pl.CostEstimate(flops=1, bytes_accessed=1, transcendentals=0)
    state_shape = jax.ShapeDtypeStruct(flow_state.shape, jnp.float32)
    sibling = [(i, i ^ 1) for i in range(lines)]
    shifts = range(2, lines, 2)

    def across(array):
        return [lax.ppermute(array, "line", [(i, (i + s) % lines) for i in range(lines)]) for s in shifts]

    low, high = FIRST
    part = pl.pallas_call(
        functools.partial(part_kernel, low),
        in_specs=[pl.BlockSpec(memory_space=pl.ANY)],
        out_specs=pl.BlockSpec(memory_space=VMEM),
        out_shape=jax.ShapeDtypeStruct((1, high - low, rows, x_length), jnp.float32),
        scratch_shapes=[pltpu.SemaphoreType.DMA(((high - low) * PIECES,))],
        compiler_params=limit,
        cost_estimate=small,
        name="part",
    )(pltpu.with_memory_space_constraint(flow_state, HBM))
    part, flow_state = lax.optimization_barrier((part, flow_state))
    direct_first = across(part)
    second = flow_state[:, SECOND[0] : SECOND[1]]
    direct_second = across(second)
    near_sent = lax.ppermute(
        jnp.concatenate([flow_state[:, v : v + 1] for v in SENT], axis=1), "line", sibling
    )

    last = x_length // LANES - 1
    faces = pl.pallas_call(
        faces_kernel,
        grid=(1,),
        in_specs=[
            smem(),
            smem(),
            pl.BlockSpec((1, nvar, rows, LANES), lambda i: (0, 0, 0, 0)),
            pl.BlockSpec((1, nvar, rows, LANES), lambda i: (0, 0, 0, last)),
        ],
        out_specs=pl.BlockSpec((1, 2, FACE_ROWS, rows), lambda i: (0, 0, 0, 0)),
        out_shape=jax.ShapeDtypeStruct((1, 2, FACE_ROWS, rows), jnp.float32),
        compiler_params=limit,
        cost_estimate=small,
        name="faces",
    )(block_owner, rows_live, flow_state, flow_state)

    w_near = jax.ShapeDtypeStruct((2 * rows, 3 * rows), jnp.bfloat16)
    w_far = jax.ShapeDtypeStruct((2 * rows, 3 * len(shifts) * rows), jnp.bfloat16)
    w_send = jax.ShapeDtypeStruct((len(shifts), 2 * rows, 6 * rows), jnp.bfloat16)
    nu = jax.ShapeDtypeStruct((nvar, 8, x_length), jnp.float32)
    w_own, w_near, w_direct, w_passed, w_send, nu = pl.pallas_call(
        functools.partial(weights_kernel, lines),
        in_specs=[smem()] * 3 + [pl.BlockSpec(memory_space=pl.ANY)],
        out_specs=[kept()] * 6,
        out_shape=[w_near, w_near, w_far, w_far, w_send, nu],
        scratch_shapes=[
            pltpu.VMEM((2, y_length, LANES), jnp.float32),
            pltpu.VMEM((2, LANES, y_length), jnp.float32),
            pltpu.VMEM((len(shifts), 2, 2 * rows, LANES), jnp.float32),
            pltpu.VMEM((lines, 2 * rows, rows), jnp.bfloat16),
            pltpu.VMEM((lines, 2 * rows, rows), jnp.bfloat16),
            pltpu.SemaphoreType.DMA((2 + 4 * len(shifts),)),
        ],
        compiler_params=limit,
        cost_estimate=small,
        name="weights",
    )(block_owner, rows_live, coefficients, pltpu.with_memory_space_constraint(y_operator, HBM))

    tiles = x_length // TILE
    def own_terms(w_own):
        return pl.pallas_call(
            own_kernel,
            grid=(tiles,),
            in_specs=[smem()] * 3
            + [
                pl.BlockSpec(w_own.shape, lambda n: (0, 0)),
                pl.BlockSpec((1, nvar, rows, x_length), lambda n: (0, 0, 0, 0)),
                pl.BlockSpec((1, nvar, rows, TILE), lambda n: (0, 0, 0, n)),
                pl.BlockSpec((x_length, TILE), lambda n: (0, n)),
                pl.BlockSpec((x_length, TILE), lambda n: (0, n + tiles)),
            ],
            out_specs=pl.BlockSpec((1, nvar, rows, TILE), lambda n: (0, 0, 0, n)),
            out_shape=state_shape,
            scratch_shapes=[
                pltpu.VMEM((nvar * rows, x_length), jnp.bfloat16),
                pltpu.VMEM((nvar * rows, x_length), jnp.bfloat16),
            ],
            compiler_params=limit,
            cost_estimate=small,
            name="own_terms",
        )(
            block_owner,
            rows_live,
            coefficients,
            w_own,
            flow_state,
            flow_state,
            *[pltpu.with_memory_space_constraint(x_operator, HBM)] * 2,
        )

    far_v = [direct_first[shifts.index(lines - s)] for s in shifts]
    sent = jax.ShapeDtypeStruct((1, len(SENT), rows, x_length), jnp.float32)
    send = pl.pallas_call(
        send_kernel,
        in_specs=[kept()] * (4 + len(shifts)),
        out_specs=[kept()] * len(shifts),
        out_shape=[sent] * len(shifts),
        compiler_params=limit,
        cost_estimate=small,
        name="send_terms",
    )
    arrived = [faces]
    held_faces, step = faces, 1
    while step < slots:
        there = lax.ppermute(held_faces, "blk", [(i, i ^ step) for i in range(slots)])
        if step == 1:
            there, w_own, own = lax.optimization_barrier((there, w_own, flow_state))
            near_raw = lax.ppermute(own[:, RAW[0] : RAW[-1] + 1], "line", sibling)
        elif step == 2:
            state = own_terms(w_own)
            w_send, *_ = lax.optimization_barrier((w_send, state, there))
            results = send(*map(held, (w_send, nu, flow_state, near_sent, *far_v)))
            direct_first, *_ = lax.optimization_barrier((direct_first, *results))
            direct_second, *_ = lax.optimization_barrier((direct_second, *results))
        arrived.append(there)
        step *= 2
        if step < slots:
            held_faces = jnp.concatenate([held_faces, there], axis=0)

    results = [
        lax.ppermute(result, "line", [(i, (i + s) % lines) for i in range(lines)])
        for s, result in zip(shifts, results)
    ]

    passed_first = [lax.ppermute(piece, "line", sibling) for piece in direct_first]
    passed_second = [lax.ppermute(piece, "line", sibling) for piece in direct_second]
    pieces = [*direct_first, *passed_first, *direct_second, *passed_second]
    state = pl.pallas_call(
        functools.partial(raw_kernel, len(shifts)),
        in_specs=[kept()] * (5 + len(pieces)),
        out_specs=kept(),
        out_shape=state_shape,
        compiler_params=limit,
        cost_estimate=small,
        name="raw_terms",
    )(*map(held, (w_direct, w_passed, nu, flow_state, state, *pieces)))

    anywhere = pl.BlockSpec(memory_space=pl.ANY)
    result, left = pl.pallas_call(
        functools.partial(near_kernel, len(arrived)),
        in_specs=[smem()] * 4 + [kept()] * (7 + len(arrived)),
        out_specs=[anywhere, kept()],
        out_shape=[state_shape, sent],
        scratch_shapes=[
            pltpu.VMEM((len(RAW), rows, x_length), jnp.float32),
            pltpu.SemaphoreType.DMA((len(RAW),)),
        ],
        compiler_params=limit,
        cost_estimate=small,
        name="near_terms",
    )(
        block_owner,
        link_block.T,
        link_side.T,
        rows_live,
        *map(held, (ghost_operator, w_near, nu, flow_state, state, near_raw, near_sent, *arrived)),
    )

    operands = [*map(held, (left, *results))]
    return pl.pallas_call(
        last_kernel,
        in_specs=[kept()] * len(operands) + [anywhere],
        out_specs=anywhere,
        out_shape=state_shape,
        input_output_aliases={len(operands): 0},
        scratch_shapes=[pltpu.VMEM(sent.shape[1:], jnp.float32), pltpu.SemaphoreType.DMA((len(SENT) * PIECES,))],
        compiler_params=limit,
        cost_estimate=small,
        name="last_terms",
    )(*operands, result)


def solution(mesh):
    return jax.shard_map(
        functools.partial(on_device, mesh.shape["blk"], mesh.shape["line"]),
        mesh=mesh,
        in_specs=(P("blk", None, "line", None), P(), P(), P(), P(), P(), P(), P(), P()),
        out_specs=P("blk", None, "line", None),
        check_vma=False,
    )
```

```python
import functools

import jax
import jax.numpy as jnp
from jax import lax
from jax.experimental import pallas as pl
from jax.experimental.pallas import tpu as pltpu
from jax.sharding import PartitionSpec as P

GHOST = 3
SECTION_STEP = 0.3
FACE_ROWS = 16
TILE = 256
LANES = 128
FIRST, SECOND = (1, 3), (3, 4)
RAW = tuple(range(FIRST[0], SECOND[1]))
SENT = (0, 4)

SMEM = pltpu.MemorySpace.SMEM
VMEM = pltpu.MemorySpace.VMEM
HBM = pltpu.MemorySpace.HBM


def split_bf16(x):
    hi = x.astype(jnp.bfloat16)
    lo = (x - hi.astype(jnp.float32)).astype(jnp.bfloat16)
    return hi, lo


def dot(a, b):
    return jnp.dot(a, b, preferred_element_type=jnp.float32)


def three_parts(pieces):
    split = [split_bf16(piece) for piece in pieces]
    hi = [s[0] for s in split]
    lo = [s[1] for s in split]
    return jnp.concatenate(hi + hi + lo, axis=0)


def find_block(owner_ref, my_slot):
    return lax.fori_loop(
        0, owner_ref.shape[0], lambda i, found: jnp.where(owner_ref[i] == my_slot, i, found), 0
    )


def faces_kernel(owner_ref, rows_ref, part_ref, q_ref, held_ref, out_ref, sems):
    nvar, rows, x_length = held_ref.shape[1:]
    copies = [pltpu.make_async_copy(q_ref.at[0, v], held_ref.at[0, v], sems.at[v]) for v in range(nvar)]
    for copy in copies:
        copy.start()
    live_rows = rows_ref[find_block(owner_ref, lax.axis_index("blk"))]
    y_index = lax.axis_index("line") * rows + lax.broadcasted_iota(jnp.int32, (GHOST, rows), 1)
    live = y_index < live_rows
    for m in range(2):
        out_ref[0, m, GHOST * nvar :, :] = jnp.zeros((FACE_ROWS - GHOST * nvar, rows), jnp.float32)
    for v in range(nvar):
        copies[v].wait()
        low = jnp.transpose(held_ref[0, v, :, :LANES])[:GHOST]
        high = jnp.transpose(held_ref[0, v, :, x_length - LANES :])[LANES - GHOST :]
        out_ref[0, 0, GHOST * v : GHOST * (v + 1), :] = jnp.where(live, low, 0.0)
        out_ref[0, 1, GHOST * v : GHOST * (v + 1), :] = jnp.where(live, high, 0.0)


def part_kernel(low, q_ref, out_ref, sem):
    copy = pltpu.make_async_copy(q_ref.at[:, low : low + out_ref.shape[1]], out_ref, sem)
    copy.start()
    copy.wait()


def weights_kernel(
    lines,
    owner_ref,
    rows_ref,
    coef_ref,
    yop_ref,
    wown_ref,
    wnear_ref,
    wdirect_ref,
    wpassed_ref,
    wsend_ref,
    nu_ref,
    columns_ref,
    turned_ref,
    theirs_ref,
    pieces_hi_ref,
    pieces_lo_ref,
    sems,
):
    y_length = yop_ref.shape[0]
    rows = y_length // lines
    line_pos = lax.axis_index("line")
    other = jnp.bitwise_xor(line_pos, 1)
    shifts = range(2, lines, 2)
    targets = [lax.rem(line_pos + s, lines) for s in shifts]

    def column(d, line):
        return pl.ds(pl.multiple_of(d * y_length + (line * rows) // LANES * LANES, LANES), LANES)

    copies = []
    for d in range(2):
        source = yop_ref.at[:, column(d, line_pos)]
        copies.append(pltpu.make_async_copy(source, columns_ref.at[d], sems.at[d]))
    for j, target in enumerate(targets):
        for d in range(2):
            for i, line in enumerate((line_pos, other)):
                source = yop_ref.at[pl.ds(pl.multiple_of(line * rows, 8), rows), column(d, target)]
                goal = theirs_ref.at[j, d, i * rows : (i + 1) * rows]
                copies.append(pltpu.make_async_copy(source, goal, sems.at[len(copies)]))
    for copy in copies:
        copy.start()

    live_rows = rows_ref[find_block(owner_ref, lax.axis_index("blk"))]
    for v in range(nu_ref.shape[0]):
        nu_ref[v] = jnp.full(nu_ref.shape[1:], coef_ref[v], jnp.float32)
    for copy in copies:
        copy.wait()

    shape = (rows, y_length)
    live_in = lax.broadcasted_iota(jnp.int32, shape, 1) < live_rows
    live_out = line_pos * rows + lax.broadcasted_iota(jnp.int32, shape, 0) < live_rows
    offset = pl.multiple_of(lax.rem(line_pos * rows, LANES), 8)
    for d in range(2):
        turned_ref[d] = jnp.transpose(columns_ref[d])
        mine = turned_ref[d, pl.ds(offset, rows), :]
        hi, lo = split_bf16(jnp.where(live_in & live_out, SECTION_STEP * mine, 0.0))
        for p in range(lines):
            pieces_hi_ref[p, d * rows : (d + 1) * rows] = hi[:, p * rows : (p + 1) * rows]
            pieces_lo_ref[p, d * rows : (d + 1) * rows] = lo[:, p * rows : (p + 1) * rows]

    def gather(ref, places):
        hi = [pieces_hi_ref[p] for p in places]
        lo = [pieces_lo_ref[p] for p in places]
        ref[...] = jnp.concatenate(hi + lo + hi, axis=1)

    gather(wown_ref, [line_pos])
    gather(wnear_ref, [other])
    gather(wdirect_ref, [lax.rem(line_pos + lines - s, lines) for s in shifts])
    gather(wpassed_ref, [lax.rem(other + lines - s, lines) for s in shifts])

    shape = (rows, rows)
    ins = [line * rows + lax.broadcasted_iota(jnp.int32, shape, 1) for line in (line_pos, other)]
    live_in = jnp.concatenate(ins, axis=1) < live_rows
    for j, target in enumerate(targets):
        live_out = target * rows + lax.broadcasted_iota(jnp.int32, live_in.shape, 0) < live_rows
        offset = pl.multiple_of(lax.rem(target * rows, LANES), 8)
        for d in range(2):
            turned_ref[d, :, : 2 * rows] = jnp.transpose(theirs_ref[j, d])
            mine = turned_ref[d, pl.ds(offset, rows), : 2 * rows]
            hi, lo = split_bf16(jnp.where(live_in & live_out, SECTION_STEP * mine, 0.0))
            wsend_ref[j, d * rows : (d + 1) * rows] = jnp.concatenate([hi, lo, hi], axis=1)


def own_kernel(
    owner_ref,
    rows_ref,
    coef_ref,
    wown_ref,
    q_ref,
    tile_ref,
    dx_ref,
    dxx_ref,
    out_ref,
    hi_ref,
    lo_ref,
):
    nvar, rows, _ = q_ref.shape[1:]
    live_rows = rows_ref[find_block(owner_ref, lax.axis_index("blk"))]

    @pl.when(pl.program_id(0) == 0)
    def _():
        for v in range(nvar):
            hi, lo = split_bf16(q_ref[0, v])
            hi_ref[v * rows : (v + 1) * rows] = hi
            lo_ref[v * rows : (v + 1) * rows] = lo

    def derivative(op_ref):
        hi, lo = split_bf16(op_ref[...])
        return dot(hi_ref[...], hi) + dot(lo_ref[...], hi) + dot(hi_ref[...], lo)

    dx = derivative(dx_ref)
    dxx = derivative(dxx_ref)
    u, w = tile_ref[0, 0], tile_ref[0, 1]
    live = lax.axis_index("line") * rows + lax.broadcasted_iota(jnp.int32, u.shape, 0) < live_rows
    for v in range(nvar):
        here = slice(v * rows, (v + 1) * rows)
        dy = dot(wown_ref[...], three_parts([tile_ref[0, v]]))
        rhs = coef_ref[v] * dxx[here] - u * dx[here]
        if v == 1:
            rhs = rhs + coef_ref[nvar] * tile_ref[0, 3] + coef_ref[nvar + 1] * tile_ref[0, 4]
        value = jnp.where(live, tile_ref[0, v] + SECTION_STEP * rhs, 0.0)
        out_ref[0, v] = value + coef_ref[v] * dy[rows:] - w * dy[:rows]


def near_kernel(
    face_count,
    owner_ref,
    link_ref,
    side_ref,
    rows_ref,
    gop_ref,
    wnear_ref,
    nu_ref,
    q_ref,
    base_ref,
    near_raw_ref,
    *refs,
):
    near_sent, refs = refs[0], refs[1:]
    faces, (out_ref, left_ref, done_ref, sems) = refs[:face_count], refs[face_count:]
    near = {v: near_sent.at[0, i] for i, v in enumerate(SENT)}
    near.update({v: near_raw_ref.at[0, i] for i, v in enumerate(RAW)})
    nvar, rows, x_length = q_ref.shape[1:]
    my_slot = lax.axis_index("blk")
    my_block = find_block(owner_ref, my_slot)
    sides = [side_ref[m, my_block] for m in range(2)]
    live_rows = rows_ref[my_block]
    y_index = lax.axis_index("line") * rows + lax.broadcasted_iota(jnp.int32, (FACE_ROWS, rows), 1)
    scale = jnp.where(y_index < live_rows, SECTION_STEP, 0.0)

    planes = []
    for m in range(2):
        place = jnp.bitwise_xor(owner_ref[link_ref[m, my_block]], my_slot)
        plane, first = faces[0][0, sides[m]], 1
        for ref in faces[1:]:
            count = ref.shape[0]
            at = jnp.clip(place - first, 0, count - 1)
            plane = jnp.where(place >= first, ref[at, sides[m]], plane)
            first += count
        planes.append(plane * scale)

    def ghost_rows(g):
        parts = []
        for m in range(2):
            straight = g[GHOST * m : GHOST * (m + 1)]
            turned = jnp.concatenate([straight[2:3], straight[1:2], straight[0:1]], axis=0)
            parts.append(jnp.where(sides[m] == m, turned, straight))
        hi, lo = split_bf16(jnp.concatenate(parts, axis=0))
        pad = jnp.zeros((LANES - 6 * GHOST, hi.shape[1]), jnp.float32)
        stacked = [hi.astype(jnp.float32), hi.astype(jnp.float32), lo.astype(jnp.float32)]
        return jnp.concatenate(stacked + [pad], axis=0).astype(jnp.bfloat16)

    operator = ghost_rows(gop_ref[...])
    pad = jnp.zeros((LANES - 6 * GHOST, rows), jnp.float32)
    copies = []
    for v in RAW + SENT:
        parts = []
        for m in range(2):
            part = planes[m][GHOST * v : GHOST * (v + 1)]
            if v == 0:
                part = jnp.where(sides[m] == m, -part, part)
            parts.append(part)
        hi, lo = split_bf16(jnp.concatenate(parts, axis=0))
        stacked = [hi.astype(jnp.float32), lo.astype(jnp.float32), hi.astype(jnp.float32)]
        ghost = jnp.transpose(jnp.concatenate(stacked + [pad], axis=0)).astype(jnp.bfloat16)
        dx = dot(ghost, operator)
        dy = dot(wnear_ref[...], three_parts([near[v][...]]))
        second = nu_ref[v, 0:1] * (dx[:, x_length:] + dy[rows:])
        value = base_ref[0, v] + second - q_ref[0, 0] * dx[:, :x_length] - q_ref[0, 1] * dy[:rows]
        if v in SENT:
            left_ref[0, SENT.index(v)] = value
            continue
        i = RAW.index(v)
        done_ref[i] = value
        copies.append(pltpu.make_async_copy(done_ref.at[i], out_ref.at[0, v], sems.at[i]))
        copies[-1].start()
    for copy in copies:
        copy.wait()


def send_kernel(wsend_ref, nu_ref, q_ref, *refs):
    count = wsend_ref.shape[0]
    near, refs = refs[0], refs[1:]
    far_v, out = refs[:count], refs[count:]
    rows = q_ref.shape[2]
    for j in range(count):
        for i, v in enumerate(SENT):
            dy = dot(wsend_ref[j], three_parts([q_ref[0, v], near[0, i]]))
            out[j][0, i] = nu_ref[v, 0:1] * dy[rows:] - far_v[j][0, 0] * dy[:rows]


def raw_kernel(count, wdirect_ref, wpassed_ref, nu_ref, q_ref, base_ref, *refs):
    out_ref = refs[-1]
    rows = q_ref.shape[2]
    first, second = [(refs[k : k + count], refs[k + count : k + 2 * count]) for k in (0, 2 * count)]
    for (low, high), (direct, passed) in ((FIRST, first), (SECOND, second)):
        for v in range(low, high):
            dy = dot(wdirect_ref[...], three_parts([piece[0, v - low] for piece in direct]))
            dy = dy + dot(wpassed_ref[...], three_parts([piece[0, v - low] for piece in passed]))
            out_ref[0, v] = base_ref[0, v] + nu_ref[v, 0:1] * dy[rows:] - q_ref[0, 1] * dy[:rows]
    for v in SENT:
        out_ref[0, v] = base_ref[0, v]


def last_kernel(left_ref, *refs):
    results, (_, out_ref, done_ref, sems) = refs[:-4], refs[-4:]
    copies = []
    for i, v in enumerate(SENT):
        done_ref[i] = left_ref[0, i] + sum(piece[0, i] for piece in results)
        copies.append(pltpu.make_async_copy(done_ref.at[i], out_ref.at[0, v], sems.at[i]))
        copies[-1].start()
    for copy in copies:
        copy.wait()


def smem():
    return pl.BlockSpec(memory_space=SMEM)


def kept():
    return pl.BlockSpec(memory_space=VMEM)


def held(array):
    return pltpu.with_memory_space_constraint(array, VMEM)


def on_device(
    slots,
    lines,
    flow_state,
    block_owner,
    link_block,
    link_side,
    rows_live,
    x_operator,
    ghost_operator,
    y_operator,
    coefficients,
):
    _, nvar, rows, x_length = flow_state.shape
    y_length = lines * rows
    limit = pltpu.CompilerParams(vmem_limit_bytes=16 * 1024 * 1024)
    small = pl.CostEstimate(flops=1, bytes_accessed=1, transcendentals=0)
    state_shape = jax.ShapeDtypeStruct(flow_state.shape, jnp.float32)
    sibling = [(i, i ^ 1) for i in range(lines)]
    shifts = range(2, lines, 2)

    def across(array):
        return [lax.ppermute(array, "line", [(i, (i + s) % lines) for i in range(lines)]) for s in shifts]

    low, high = FIRST
    part = pl.pallas_call(
        functools.partial(part_kernel, low),
        in_specs=[pl.BlockSpec(memory_space=pl.ANY)],
        out_specs=pl.BlockSpec(memory_space=VMEM),
        out_shape=jax.ShapeDtypeStruct((1, high - low, rows, x_length), jnp.float32),
        scratch_shapes=[pltpu.SemaphoreType.DMA],
        compiler_params=limit,
        cost_estimate=small,
        name="part",
    )(pltpu.with_memory_space_constraint(flow_state, HBM))
    direct_first = across(part)

    in_hbm = pltpu.with_memory_space_constraint(flow_state, HBM)
    flow_state, faces = pl.pallas_call(
        faces_kernel,
        in_specs=[smem(), smem(), kept(), pl.BlockSpec(memory_space=pl.ANY)],
        out_specs=[kept(), kept()],
        out_shape=[state_shape, jax.ShapeDtypeStruct((1, 2, FACE_ROWS, rows), jnp.float32)],
        scratch_shapes=[pltpu.SemaphoreType.DMA((nvar,))],
        compiler_params=limit,
        cost_estimate=small,
        name="faces",
    )(block_owner, rows_live, held(part), in_hbm)
    second = flow_state[:, SECOND[0] : SECOND[1]]
    direct_second = across(second)
    near_sent = lax.ppermute(
        jnp.concatenate([flow_state[:, v : v + 1] for v in SENT], axis=1), "line", sibling
    )

    w_near = jax.ShapeDtypeStruct((2 * rows, 3 * rows), jnp.bfloat16)
    w_far = jax.ShapeDtypeStruct((2 * rows, 3 * len(shifts) * rows), jnp.bfloat16)
    w_send = jax.ShapeDtypeStruct((len(shifts), 2 * rows, 6 * rows), jnp.bfloat16)
    nu = jax.ShapeDtypeStruct((nvar, 8, x_length), jnp.float32)
    w_own, w_near, w_direct, w_passed, w_send, nu = pl.pallas_call(
        functools.partial(weights_kernel, lines),
        in_specs=[smem()] * 3 + [pl.BlockSpec(memory_space=pl.ANY)],
        out_specs=[kept()] * 6,
        out_shape=[w_near, w_near, w_far, w_far, w_send, nu],
        scratch_shapes=[
            pltpu.VMEM((2, y_length, LANES), jnp.float32),
            pltpu.VMEM((2, LANES, y_length), jnp.float32),
            pltpu.VMEM((len(shifts), 2, 2 * rows, LANES), jnp.float32),
            pltpu.VMEM((lines, 2 * rows, rows), jnp.bfloat16),
            pltpu.VMEM((lines, 2 * rows, rows), jnp.bfloat16),
            pltpu.SemaphoreType.DMA((2 + 4 * len(shifts),)),
        ],
        compiler_params=limit,
        cost_estimate=small,
        name="weights",
    )(block_owner, rows_live, coefficients, pltpu.with_memory_space_constraint(y_operator, HBM))

    tiles = x_length // TILE
    def own_terms(w_own):
        return pl.pallas_call(
            own_kernel,
            grid=(tiles,),
            in_specs=[smem()] * 3
            + [
                pl.BlockSpec(w_own.shape, lambda n: (0, 0)),
                pl.BlockSpec((1, nvar, rows, x_length), lambda n: (0, 0, 0, 0)),
                pl.BlockSpec((1, nvar, rows, TILE), lambda n: (0, 0, 0, n)),
                pl.BlockSpec((x_length, TILE), lambda n: (0, n)),
                pl.BlockSpec((x_length, TILE), lambda n: (0, n + tiles)),
            ],
            out_specs=pl.BlockSpec((1, nvar, rows, TILE), lambda n: (0, 0, 0, n)),
            out_shape=state_shape,
            scratch_shapes=[
                pltpu.VMEM((nvar * rows, x_length), jnp.bfloat16),
                pltpu.VMEM((nvar * rows, x_length), jnp.bfloat16),
            ],
            compiler_params=limit,
            cost_estimate=small,
            name="own_terms",
        )(
            block_owner,
            rows_live,
            coefficients,
            w_own,
            flow_state,
            flow_state,
            *[pltpu.with_memory_space_constraint(x_operator, HBM)] * 2,
        )

    far_v = [direct_first[shifts.index(lines - s)] for s in shifts]
    sent = jax.ShapeDtypeStruct((1, len(SENT), rows, x_length), jnp.float32)
    send = pl.pallas_call(
        send_kernel,
        in_specs=[kept()] * (4 + len(shifts)),
        out_specs=[kept()] * len(shifts),
        out_shape=[sent] * len(shifts),
        compiler_params=limit,
        cost_estimate=small,
        name="send_terms",
    )
    arrived = [faces]
    held_faces, step = faces, 1
    while step < slots:
        there = lax.ppermute(held_faces, "blk", [(i, i ^ step) for i in range(slots)])
        if step == 1:
            there, w_own, own = lax.optimization_barrier((there, w_own, flow_state))
            near_raw = lax.ppermute(own[:, RAW[0] : RAW[-1] + 1], "line", sibling)
        elif step == 2:
            state = own_terms(w_own)
            w_send, *_ = lax.optimization_barrier((w_send, state, there))
            results = send(*map(held, (w_send, nu, flow_state, near_sent, *far_v)))
            direct_first, *_ = lax.optimization_barrier((direct_first, *results))
            direct_second, *_ = lax.optimization_barrier((direct_second, *results))
        arrived.append(there)
        step *= 2
        if step < slots:
            held_faces = jnp.concatenate([held_faces, there], axis=0)

    results = [
        lax.ppermute(result, "line", [(i, (i + s) % lines) for i in range(lines)])
        for s, result in zip(shifts, results)
    ]

    direct_second, *_ = lax.optimization_barrier((direct_second, *arrived))
    passed_first = [lax.ppermute(piece, "line", sibling) for piece in direct_first]
    passed_second = [lax.ppermute(piece, "line", sibling) for piece in direct_second]
    pieces = [*direct_first, *passed_first, *direct_second, *passed_second]
    state = pl.pallas_call(
        functools.partial(raw_kernel, len(shifts)),
        in_specs=[kept()] * (5 + len(pieces)),
        out_specs=kept(),
        out_shape=state_shape,
        compiler_params=limit,
        cost_estimate=small,
        name="raw_terms",
    )(*map(held, (w_direct, w_passed, nu, flow_state, state, *pieces)))

    anywhere = pl.BlockSpec(memory_space=pl.ANY)
    result, left = pl.pallas_call(
        functools.partial(near_kernel, len(arrived)),
        in_specs=[smem()] * 4 + [kept()] * (7 + len(arrived)),
        out_specs=[anywhere, kept()],
        out_shape=[state_shape, sent],
        scratch_shapes=[
            pltpu.VMEM((len(RAW), rows, x_length), jnp.float32),
            pltpu.SemaphoreType.DMA((len(RAW),)),
        ],
        compiler_params=limit,
        cost_estimate=small,
        name="near_terms",
    )(
        block_owner,
        link_block.T,
        link_side.T,
        rows_live,
        *map(held, (ghost_operator, w_near, nu, flow_state, state, near_raw, near_sent, *arrived)),
    )

    operands = [*map(held, (left, *results))]
    return pl.pallas_call(
        last_kernel,
        in_specs=[kept()] * len(operands) + [anywhere],
        out_specs=anywhere,
        out_shape=state_shape,
        input_output_aliases={len(operands): 0},
        scratch_shapes=[pltpu.VMEM(sent.shape[1:], jnp.float32), pltpu.SemaphoreType.DMA((len(SENT),))],
        compiler_params=limit,
        cost_estimate=small,
        name="last_terms",
    )(*operands, result)


def solution(mesh):
    return jax.shard_map(
        functools.partial(on_device, mesh.shape["blk"], mesh.shape["line"]),
        mesh=mesh,
        in_specs=(P("blk", None, "line", None), P(), P(), P(), P(), P(), P(), P(), P()),
        out_specs=P("blk", None, "line", None),
        check_vma=False,
    )
```

```python
import functools

import jax
import jax.numpy as jnp
from jax import lax
from jax.experimental import pallas as pl
from jax.experimental.pallas import tpu as pltpu
from jax.sharding import PartitionSpec as P

GHOST = 3
SECTION_STEP = 0.3
FACE_ROWS = 16
TILE = 256
LANES = 128
FIRST, SECOND = (1, 3), (3, 4)
RAW = tuple(range(FIRST[0], SECOND[1]))
SENT = (0, 4)

SMEM = pltpu.MemorySpace.SMEM
VMEM = pltpu.MemorySpace.VMEM
HBM = pltpu.MemorySpace.HBM


def split_bf16(x):
    hi = x.astype(jnp.bfloat16)
    lo = (x - hi.astype(jnp.float32)).astype(jnp.bfloat16)
    return hi, lo


def dot(a, b):
    return jnp.dot(a, b, preferred_element_type=jnp.float32)


def three_parts(pieces):
    split = [split_bf16(piece) for piece in pieces]
    hi = [s[0] for s in split]
    lo = [s[1] for s in split]
    return jnp.concatenate(hi + hi + lo, axis=0)


def find_block(owner_ref, my_slot):
    return lax.fori_loop(
        0, owner_ref.shape[0], lambda i, found: jnp.where(owner_ref[i] == my_slot, i, found), 0
    )


def faces_kernel(owner_ref, rows_ref, part_ref, q_ref, held_ref, out_ref, sems):
    nvar, rows, x_length = held_ref.shape[1:]
    copies = [pltpu.make_async_copy(q_ref.at[0, v], held_ref.at[0, v], sems.at[v]) for v in range(nvar)]
    for copy in copies:
        copy.start()
    live_rows = rows_ref[find_block(owner_ref, lax.axis_index("blk"))]
    y_index = lax.axis_index("line") * rows + lax.broadcasted_iota(jnp.int32, (GHOST, rows), 1)
    live = y_index < live_rows
    for m in range(2):
        out_ref[0, m, GHOST * nvar :, :] = jnp.zeros((FACE_ROWS - GHOST * nvar, rows), jnp.float32)
    for v in range(nvar):
        copies[v].wait()
        low = jnp.transpose(held_ref[0, v, :, :LANES])[:GHOST]
        high = jnp.transpose(held_ref[0, v, :, x_length - LANES :])[LANES - GHOST :]
        out_ref[0, 0, GHOST * v : GHOST * (v + 1), :] = jnp.where(live, low, 0.0)
        out_ref[0, 1, GHOST * v : GHOST * (v + 1), :] = jnp.where(live, high, 0.0)


def part_kernel(low, q_ref, out_ref, sem):
    copy = pltpu.make_async_copy(q_ref.at[:, low : low + out_ref.shape[1]], out_ref, sem)
    copy.start()
    copy.wait()


def weights_kernel(
    lines,
    owner_ref,
    rows_ref,
    coef_ref,
    yop_ref,
    wown_ref,
    wnear_ref,
    wdirect_ref,
    wsibling_ref,
    wsend_ref,
    nu_ref,
    columns_ref,
    turned_ref,
    theirs_ref,
    pieces_hi_ref,
    pieces_lo_ref,
    sems,
):
    y_length = yop_ref.shape[0]
    rows = y_length // lines
    line_pos = lax.axis_index("line")
    other = jnp.bitwise_xor(line_pos, 1)
    shifts = range(2, lines, 2)
    targets = [lax.rem(line_pos + s, lines) for s in shifts]

    def column(d, line):
        return pl.ds(pl.multiple_of(d * y_length + (line * rows) // LANES * LANES, LANES), LANES)

    copies = []
    for d in range(2):
        source = yop_ref.at[:, column(d, line_pos)]
        copies.append(pltpu.make_async_copy(source, columns_ref.at[d], sems.at[d]))
    direct = [lax.rem(line_pos + lines - s, lines) for s in shifts]
    others = [(target, [line_pos, other]) for target in targets] + [(other, [line_pos] + direct)]
    for j, (target, sources) in enumerate(others):
        for d in range(2):
            for i, line in enumerate(sources):
                source = yop_ref.at[pl.ds(pl.multiple_of(line * rows, 8), rows), column(d, target)]
                goal = theirs_ref.at[j, d, i * rows : (i + 1) * rows]
                copies.append(pltpu.make_async_copy(source, goal, sems.at[len(copies)]))
    for copy in copies:
        copy.start()

    live_rows = rows_ref[find_block(owner_ref, lax.axis_index("blk"))]
    for v in range(nu_ref.shape[0]):
        nu_ref[v] = jnp.full(nu_ref.shape[1:], coef_ref[v], jnp.float32)
    for copy in copies:
        copy.wait()

    shape = (rows, y_length)
    live_in = lax.broadcasted_iota(jnp.int32, shape, 1) < live_rows
    live_out = line_pos * rows + lax.broadcasted_iota(jnp.int32, shape, 0) < live_rows
    offset = pl.multiple_of(lax.rem(line_pos * rows, LANES), 8)
    for d in range(2):
        turned_ref[d] = jnp.transpose(columns_ref[d])
        mine = turned_ref[d, pl.ds(offset, rows), :]
        hi, lo = split_bf16(jnp.where(live_in & live_out, SECTION_STEP * mine, 0.0))
        for p in range(lines):
            pieces_hi_ref[p, d * rows : (d + 1) * rows] = hi[:, p * rows : (p + 1) * rows]
            pieces_lo_ref[p, d * rows : (d + 1) * rows] = lo[:, p * rows : (p + 1) * rows]

    def gather(ref, places):
        hi = [pieces_hi_ref[p] for p in places]
        lo = [pieces_lo_ref[p] for p in places]
        ref[...] = jnp.concatenate(hi + lo + hi, axis=1)

    gather(wown_ref, [line_pos])
    gather(wnear_ref, [other])
    gather(wdirect_ref, direct)

    for j, (target, sources) in enumerate(others):
        depth = len(sources) * rows
        shape = (rows, rows)
        ins = [line * rows + lax.broadcasted_iota(jnp.int32, shape, 1) for line in sources]
        live_in = jnp.concatenate(ins, axis=1) < live_rows
        live_out = target * rows + lax.broadcasted_iota(jnp.int32, live_in.shape, 0) < live_rows
        offset = pl.multiple_of(lax.rem(target * rows, LANES), 8)
        goal = wsend_ref.at[j] if j < len(targets) else wsibling_ref
        for d in range(2):
            turned_ref[d, :, :depth] = jnp.transpose(theirs_ref[j, d, :depth])
            mine = turned_ref[d, pl.ds(offset, rows), :depth]
            hi, lo = split_bf16(jnp.where(live_in & live_out, SECTION_STEP * mine, 0.0))
            goal[d * rows : (d + 1) * rows] = jnp.concatenate([hi, lo, hi], axis=1)


def own_kernel(
    owner_ref,
    rows_ref,
    coef_ref,
    wown_ref,
    q_ref,
    tile_ref,
    dx_ref,
    dxx_ref,
    out_ref,
    hi_ref,
    lo_ref,
):
    nvar, rows, _ = q_ref.shape[1:]
    live_rows = rows_ref[find_block(owner_ref, lax.axis_index("blk"))]

    @pl.when(pl.program_id(0) == 0)
    def _():
        for v in range(nvar):
            hi, lo = split_bf16(q_ref[0, v])
            hi_ref[v * rows : (v + 1) * rows] = hi
            lo_ref[v * rows : (v + 1) * rows] = lo

    def derivative(op_ref):
        hi, lo = split_bf16(op_ref[...])
        return dot(hi_ref[...], hi) + dot(lo_ref[...], hi) + dot(hi_ref[...], lo)

    dx = derivative(dx_ref)
    dxx = derivative(dxx_ref)
    u, w = tile_ref[0, 0], tile_ref[0, 1]
    live = lax.axis_index("line") * rows + lax.broadcasted_iota(jnp.int32, u.shape, 0) < live_rows
    for v in range(nvar):
        here = slice(v * rows, (v + 1) * rows)
        dy = dot(wown_ref[...], three_parts([tile_ref[0, v]]))
        rhs = coef_ref[v] * dxx[here] - u * dx[here]
        if v == 1:
            rhs = rhs + coef_ref[nvar] * tile_ref[0, 3] + coef_ref[nvar + 1] * tile_ref[0, 4]
        value = jnp.where(live, tile_ref[0, v] + SECTION_STEP * rhs, 0.0)
        out_ref[0, v] = value + coef_ref[v] * dy[rows:] - w * dy[:rows]


def near_kernel(
    face_count,
    owner_ref,
    link_ref,
    side_ref,
    rows_ref,
    gop_ref,
    wnear_ref,
    wdirect_ref,
    nu_ref,
    q_ref,
    base_ref,
    near_ref,
    *refs,
):
    faces, refs = refs[:face_count], refs[face_count:]
    *refs, out_ref, left_ref, done_ref, sems = refs
    count = len(refs) // 2 - 1
    raw = {}
    for (low, high), parts in ((FIRST, refs[: count + 1]), (SECOND, refs[count + 1 :])):
        for v in range(low, high):
            raw[v] = [ref.at[0, v - low] for ref in parts]
    nvar, rows, x_length = q_ref.shape[1:]
    my_slot = lax.axis_index("blk")
    my_block = find_block(owner_ref, my_slot)
    sides = [side_ref[m, my_block] for m in range(2)]
    live_rows = rows_ref[my_block]
    y_index = lax.axis_index("line") * rows + lax.broadcasted_iota(jnp.int32, (FACE_ROWS, rows), 1)
    scale = jnp.where(y_index < live_rows, SECTION_STEP, 0.0)

    planes = []
    for m in range(2):
        place = jnp.bitwise_xor(owner_ref[link_ref[m, my_block]], my_slot)
        plane, first = faces[0][0, sides[m]], 1
        for ref in faces[1:]:
            count = ref.shape[0]
            at = jnp.clip(place - first, 0, count - 1)
            plane = jnp.where(place >= first, ref[at, sides[m]], plane)
            first += count
        planes.append(plane * scale)

    def ghost_rows(g):
        parts = []
        for m in range(2):
            straight = g[GHOST * m : GHOST * (m + 1)]
            turned = jnp.concatenate([straight[2:3], straight[1:2], straight[0:1]], axis=0)
            parts.append(jnp.where(sides[m] == m, turned, straight))
        hi, lo = split_bf16(jnp.concatenate(parts, axis=0))
        pad = jnp.zeros((LANES - 6 * GHOST, hi.shape[1]), jnp.float32)
        stacked = [hi.astype(jnp.float32), hi.astype(jnp.float32), lo.astype(jnp.float32)]
        return jnp.concatenate(stacked + [pad], axis=0).astype(jnp.bfloat16)

    operator = ghost_rows(gop_ref[...])
    pad = jnp.zeros((LANES - 6 * GHOST, rows), jnp.float32)
    copies = []
    for v in RAW + SENT:
        parts = []
        for m in range(2):
            part = planes[m][GHOST * v : GHOST * (v + 1)]
            if v == 0:
                part = jnp.where(sides[m] == m, -part, part)
            parts.append(part)
        hi, lo = split_bf16(jnp.concatenate(parts, axis=0))
        stacked = [hi.astype(jnp.float32), lo.astype(jnp.float32), hi.astype(jnp.float32)]
        ghost = jnp.transpose(jnp.concatenate(stacked + [pad], axis=0)).astype(jnp.bfloat16)
        dx = dot(ghost, operator)
        if v in SENT:
            dy = dot(wnear_ref[...], three_parts([near_ref[0, SENT.index(v)]]))
        else:
            *direct, from_sibling = raw[v]
            dy = dot(wdirect_ref[...], three_parts([ref[...] for ref in direct]))
        second = nu_ref[v, 0:1] * (dx[:, x_length:] + dy[rows:])
        value = base_ref[0, v] + second - q_ref[0, 0] * dx[:, :x_length] - q_ref[0, 1] * dy[:rows]
        if v in SENT:
            left_ref[0, SENT.index(v)] = value
            continue
        i = RAW.index(v)
        done_ref[i] = value + from_sibling[...]
        copies.append(pltpu.make_async_copy(done_ref.at[i], out_ref.at[0, v], sems.at[i]))
        copies[-1].start()
    for copy in copies:
        copy.wait()


def send_kernel(wsend_ref, nu_ref, q_ref, *refs):
    count = wsend_ref.shape[0]
    near, refs = refs[0], refs[1:]
    far_v, out = refs[:count], refs[count:]
    rows = q_ref.shape[2]
    for j in range(count):
        for i, v in enumerate(SENT):
            dy = dot(wsend_ref[j], three_parts([q_ref[0, v], near[0, i]]))
            out[j][0, i] = nu_ref[v, 0:1] * dy[rows:] - far_v[j][0, 0] * dy[:rows]


def sibling_kernel(low, high, w_ref, nu_ref, q_ref, near_v_ref, *refs):
    direct, out_ref = refs[:-1], refs[-1]
    rows = q_ref.shape[2]
    for i in range(high - low):
        v = low + i
        dy = dot(w_ref[...], three_parts([q_ref[0, v]] + [piece[0, i] for piece in direct]))
        out_ref[0, i] = nu_ref[v, 0:1] * dy[rows:] - near_v_ref[0, 0] * dy[:rows]


def last_kernel(left_ref, *refs):
    results, (_, out_ref, done_ref, sems) = refs[:-4], refs[-4:]
    copies = []
    for i, v in enumerate(SENT):
        done_ref[i] = left_ref[0, i] + sum(piece[0, i] for piece in results)
        copies.append(pltpu.make_async_copy(done_ref.at[i], out_ref.at[0, v], sems.at[i]))
        copies[-1].start()
    for copy in copies:
        copy.wait()


def smem():
    return pl.BlockSpec(memory_space=SMEM)


def kept():
    return pl.BlockSpec(memory_space=VMEM)


def held(array):
    return pltpu.with_memory_space_constraint(array, VMEM)


def on_device(
    slots,
    lines,
    flow_state,
    block_owner,
    link_block,
    link_side,
    rows_live,
    x_operator,
    ghost_operator,
    y_operator,
    coefficients,
):
    _, nvar, rows, x_length = flow_state.shape
    y_length = lines * rows
    limit = pltpu.CompilerParams(vmem_limit_bytes=16 * 1024 * 1024)
    small = pl.CostEstimate(flops=1, bytes_accessed=1, transcendentals=0)
    state_shape = jax.ShapeDtypeStruct(flow_state.shape, jnp.float32)
    sibling = [(i, i ^ 1) for i in range(lines)]
    shifts = range(2, lines, 2)

    def across(array):
        return [lax.ppermute(array, "line", [(i, (i + s) % lines) for i in range(lines)]) for s in shifts]

    low, high = FIRST
    part = pl.pallas_call(
        functools.partial(part_kernel, low),
        in_specs=[pl.BlockSpec(memory_space=pl.ANY)],
        out_specs=pl.BlockSpec(memory_space=VMEM),
        out_shape=jax.ShapeDtypeStruct((1, high - low, rows, x_length), jnp.float32),
        scratch_shapes=[pltpu.SemaphoreType.DMA],
        compiler_params=limit,
        cost_estimate=small,
        name="part",
    )(pltpu.with_memory_space_constraint(flow_state, HBM))
    direct_first = across(part)

    in_hbm = pltpu.with_memory_space_constraint(flow_state, HBM)
    flow_state, faces = pl.pallas_call(
        faces_kernel,
        in_specs=[smem(), smem(), kept(), pl.BlockSpec(memory_space=pl.ANY)],
        out_specs=[kept(), kept()],
        out_shape=[state_shape, jax.ShapeDtypeStruct((1, 2, FACE_ROWS, rows), jnp.float32)],
        scratch_shapes=[pltpu.SemaphoreType.DMA((nvar,))],
        compiler_params=limit,
        cost_estimate=small,
        name="faces",
    )(block_owner, rows_live, held(part), in_hbm)
    second = flow_state[:, SECOND[0] : SECOND[1]]
    direct_second = across(second)
    near = lax.ppermute(
        jnp.concatenate([flow_state[:, v : v + 1] for v in SENT], axis=1), "line", sibling
    )

    w_near = jax.ShapeDtypeStruct((2 * rows, 3 * rows), jnp.bfloat16)
    w_far = jax.ShapeDtypeStruct((2 * rows, 3 * len(shifts) * rows), jnp.bfloat16)
    w_sibling = jax.ShapeDtypeStruct((2 * rows, 3 * (1 + len(shifts)) * rows), jnp.bfloat16)
    w_send = jax.ShapeDtypeStruct((len(shifts), 2 * rows, 6 * rows), jnp.bfloat16)
    nu = jax.ShapeDtypeStruct((nvar, 8, x_length), jnp.float32)
    w_own, w_near, w_direct, w_sibling, w_send, nu = pl.pallas_call(
        functools.partial(weights_kernel, lines),
        in_specs=[smem()] * 3 + [pl.BlockSpec(memory_space=pl.ANY)],
        out_specs=[kept()] * 6,
        out_shape=[w_near, w_near, w_far, w_sibling, w_send, nu],
        scratch_shapes=[
            pltpu.VMEM((2, y_length, LANES), jnp.float32),
            pltpu.VMEM((2, LANES, y_length), jnp.float32),
            pltpu.VMEM((len(shifts) + 1, 2, max(2, lines // 2) * rows, LANES), jnp.float32),
            pltpu.VMEM((lines, 2 * rows, rows), jnp.bfloat16),
            pltpu.VMEM((lines, 2 * rows, rows), jnp.bfloat16),
            pltpu.SemaphoreType.DMA((2 + 4 * len(shifts) + lines,)),
        ],
        compiler_params=limit,
        cost_estimate=small,
        name="weights",
    )(block_owner, rows_live, coefficients, pltpu.with_memory_space_constraint(y_operator, HBM))

    tiles = x_length // TILE
    def own_terms(w_own):
        return pl.pallas_call(
            own_kernel,
            grid=(tiles,),
            in_specs=[smem()] * 3
            + [
                pl.BlockSpec(w_own.shape, lambda n: (0, 0)),
                pl.BlockSpec((1, nvar, rows, x_length), lambda n: (0, 0, 0, 0)),
                pl.BlockSpec((1, nvar, rows, TILE), lambda n: (0, 0, 0, n)),
                pl.BlockSpec((x_length, TILE), lambda n: (0, n)),
                pl.BlockSpec((x_length, TILE), lambda n: (0, n + tiles)),
            ],
            out_specs=pl.BlockSpec((1, nvar, rows, TILE), lambda n: (0, 0, 0, n)),
            out_shape=state_shape,
            scratch_shapes=[
                pltpu.VMEM((nvar * rows, x_length), jnp.bfloat16),
                pltpu.VMEM((nvar * rows, x_length), jnp.bfloat16),
            ],
            compiler_params=limit,
            cost_estimate=small,
            name="own_terms",
        )(
            block_owner,
            rows_live,
            coefficients,
            w_own,
            flow_state,
            flow_state,
            *[pltpu.with_memory_space_constraint(x_operator, HBM)] * 2,
        )

    far_v = [direct_first[shifts.index(lines - s)] for s in shifts]
    sent = jax.ShapeDtypeStruct((1, len(SENT), rows, x_length), jnp.float32)
    send = pl.pallas_call(
        send_kernel,
        in_specs=[kept()] * (4 + len(shifts)),
        out_specs=[kept()] * len(shifts),
        out_shape=[sent] * len(shifts),
        compiler_params=limit,
        cost_estimate=small,
        name="send_terms",
    )
    arrived = [faces]
    held_faces, step = faces, 1
    while step < slots:
        there = lax.ppermute(held_faces, "blk", [(i, i ^ step) for i in range(slots)])
        if step == 1:
            there, w_own, own = lax.optimization_barrier((there, w_own, flow_state))
            near_v = lax.ppermute(own[:, 1:2], "line", sibling)
        elif step == 2:
            state = own_terms(w_own)
            w_send, *_ = lax.optimization_barrier((w_send, state, there))
            results = send(*map(held, (w_send, nu, flow_state, near, *far_v)))
            direct_first, *_ = lax.optimization_barrier((direct_first, *results))
            direct_second, *_ = lax.optimization_barrier((direct_second, *results))
        arrived.append(there)
        step *= 2
        if step < slots:
            held_faces = jnp.concatenate([held_faces, there], axis=0)

    results = [
        lax.ppermute(result, "line", [(i, (i + s) % lines) for i in range(lines)])
        for s, result in zip(shifts, results)
    ]

    def sibling_terms(part, direct):
        operands = [*map(held, (w_sibling, nu, flow_state, near_v, *direct))]
        low, high = part
        result = pl.pallas_call(
            functools.partial(sibling_kernel, low, high),
            in_specs=[kept()] * len(operands),
            out_specs=kept(),
            out_shape=jax.ShapeDtypeStruct((1, high - low, rows, x_length), jnp.float32),
            compiler_params=limit,
            cost_estimate=small,
            name="sibling_terms",
        )(*operands)
        return [*direct, lax.ppermute(result, "line", sibling)]

    direct_second, *_ = lax.optimization_barrier((direct_second, *arrived))
    pieces = sibling_terms(FIRST, direct_first) + sibling_terms(SECOND, direct_second)

    anywhere = pl.BlockSpec(memory_space=pl.ANY)
    result, left = pl.pallas_call(
        functools.partial(near_kernel, len(arrived)),
        in_specs=[smem()] * 4 + [kept()] * (7 + len(arrived) + len(pieces)),
        out_specs=[anywhere, kept()],
        out_shape=[state_shape, sent],
        scratch_shapes=[
            pltpu.VMEM((len(RAW), rows, x_length), jnp.float32),
            pltpu.SemaphoreType.DMA((len(RAW),)),
        ],
        compiler_params=limit,
        cost_estimate=small,
        name="near_terms",
    )(
        block_owner,
        link_block.T,
        link_side.T,
        rows_live,
        *map(held, (ghost_operator, w_near, w_direct, nu, flow_state, state, near, *arrived, *pieces)),
    )

    operands = [*map(held, (left, *results))]
    return pl.pallas_call(
        last_kernel,
        in_specs=[kept()] * len(operands) + [anywhere],
        out_specs=anywhere,
        out_shape=state_shape,
        input_output_aliases={len(operands): 0},
        scratch_shapes=[pltpu.VMEM(sent.shape[1:], jnp.float32), pltpu.SemaphoreType.DMA((len(SENT),))],
        compiler_params=limit,
        cost_estimate=small,
        name="last_terms",
    )(*operands, result)


def solution(mesh):
    return jax.shard_map(
        functools.partial(on_device, mesh.shape["blk"], mesh.shape["line"]),
        mesh=mesh,
        in_specs=(P("blk", None, "line", None), P(), P(), P(), P(), P(), P(), P(), P()),
        out_specs=P("blk", None, "line", None),
        check_vma=False,
    )
```

```python
import functools

import jax
import jax.numpy as jnp
from jax import lax
from jax.experimental import pallas as pl
from jax.experimental.pallas import tpu as pltpu
from jax.sharding import PartitionSpec as P

GHOST = 3
SECTION_STEP = 0.3
FACE_ROWS = 16
TILE = 256
LANES = 128
FIRST, SECOND = (1, 3), (3, 4)
RAW = tuple(range(FIRST[0], SECOND[1]))
SENT = (0, 4)

SMEM = pltpu.MemorySpace.SMEM
VMEM = pltpu.MemorySpace.VMEM
HBM = pltpu.MemorySpace.HBM


def split_bf16(x):
    hi = x.astype(jnp.bfloat16)
    lo = (x - hi.astype(jnp.float32)).astype(jnp.bfloat16)
    return hi, lo


def dot(a, b):
    return jnp.dot(a, b, preferred_element_type=jnp.float32)


def three_parts(pieces):
    split = [split_bf16(piece) for piece in pieces]
    hi = [s[0] for s in split]
    lo = [s[1] for s in split]
    return jnp.concatenate(hi + hi + lo, axis=0)


def find_block(owner_ref, my_slot):
    return lax.fori_loop(
        0, owner_ref.shape[0], lambda i, found: jnp.where(owner_ref[i] == my_slot, i, found), 0
    )


def faces_kernel(owner_ref, rows_ref, part_ref, q_ref, held_ref, out_ref, sems):
    nvar, rows, x_length = held_ref.shape[1:]
    copies = [pltpu.make_async_copy(q_ref.at[0, v], held_ref.at[0, v], sems.at[v]) for v in range(nvar)]
    for copy in copies:
        copy.start()
    live_rows = rows_ref[find_block(owner_ref, lax.axis_index("blk"))]
    y_index = lax.axis_index("line") * rows + lax.broadcasted_iota(jnp.int32, (GHOST, rows), 1)
    live = y_index < live_rows
    for m in range(2):
        out_ref[0, m, GHOST * nvar :, :] = jnp.zeros((FACE_ROWS - GHOST * nvar, rows), jnp.float32)
    for v in range(nvar):
        copies[v].wait()
        low = jnp.transpose(held_ref[0, v, :, :LANES])[:GHOST]
        high = jnp.transpose(held_ref[0, v, :, x_length - LANES :])[LANES - GHOST :]
        out_ref[0, 0, GHOST * v : GHOST * (v + 1), :] = jnp.where(live, low, 0.0)
        out_ref[0, 1, GHOST * v : GHOST * (v + 1), :] = jnp.where(live, high, 0.0)


def part_kernel(low, q_ref, out_ref, sem):
    copy = pltpu.make_async_copy(q_ref.at[:, low : low + out_ref.shape[1]], out_ref, sem)
    copy.start()
    copy.wait()


def weights_kernel(
    lines,
    owner_ref,
    rows_ref,
    coef_ref,
    yop_ref,
    wown_ref,
    wnear_ref,
    wdirect_ref,
    wpassed_ref,
    wsend_ref,
    nu_ref,
    columns_ref,
    turned_ref,
    theirs_ref,
    pieces_hi_ref,
    pieces_lo_ref,
    sems,
):
    y_length = yop_ref.shape[0]
    rows = y_length // lines
    line_pos = lax.axis_index("line")
    other = jnp.bitwise_xor(line_pos, 1)
    shifts = range(2, lines, 2)
    targets = [lax.rem(line_pos + s, lines) for s in shifts]

    def column(d, line):
        return pl.ds(pl.multiple_of(d * y_length + (line * rows) // LANES * LANES, LANES), LANES)

    copies = []
    for d in range(2):
        source = yop_ref.at[:, column(d, line_pos)]
        copies.append(pltpu.make_async_copy(source, columns_ref.at[d], sems.at[d]))
    for j, target in enumerate(targets):
        for d in range(2):
            for i, line in enumerate((line_pos, other)):
                source = yop_ref.at[pl.ds(pl.multiple_of(line * rows, 8), rows), column(d, target)]
                goal = theirs_ref.at[j, d, i * rows : (i + 1) * rows]
                copies.append(pltpu.make_async_copy(source, goal, sems.at[len(copies)]))
    for copy in copies:
        copy.start()

    live_rows = rows_ref[find_block(owner_ref, lax.axis_index("blk"))]
    for v in range(nu_ref.shape[0]):
        nu_ref[v] = jnp.full(nu_ref.shape[1:], coef_ref[v], jnp.float32)
    for copy in copies:
        copy.wait()

    shape = (rows, y_length)
    live_in = lax.broadcasted_iota(jnp.int32, shape, 1) < live_rows
    live_out = line_pos * rows + lax.broadcasted_iota(jnp.int32, shape, 0) < live_rows
    offset = pl.multiple_of(lax.rem(line_pos * rows, LANES), 8)
    for d in range(2):
        turned_ref[d] = jnp.transpose(columns_ref[d])
        mine = turned_ref[d, pl.ds(offset, rows), :]
        hi, lo = split_bf16(jnp.where(live_in & live_out, SECTION_STEP * mine, 0.0))
        for p in range(lines):
            pieces_hi_ref[p, d * rows : (d + 1) * rows] = hi[:, p * rows : (p + 1) * rows]
            pieces_lo_ref[p, d * rows : (d + 1) * rows] = lo[:, p * rows : (p + 1) * rows]

    def gather(ref, places):
        hi = [pieces_hi_ref[p] for p in places]
        lo = [pieces_lo_ref[p] for p in places]
        ref[...] = jnp.concatenate(hi + lo + hi, axis=1)

    gather(wown_ref, [line_pos])
    gather(wnear_ref, [other])
    gather(wdirect_ref, [lax.rem(line_pos + lines - s, lines) for s in shifts])
    gather(wpassed_ref, [lax.rem(other + lines - s, lines) for s in shifts])

    shape = (rows, rows)
    ins = [line * rows + lax.broadcasted_iota(jnp.int32, shape, 1) for line in (line_pos, other)]
    live_in = jnp.concatenate(ins, axis=1) < live_rows
    for j, target in enumerate(targets):
        live_out = target * rows + lax.broadcasted_iota(jnp.int32, live_in.shape, 0) < live_rows
        offset = pl.multiple_of(lax.rem(target * rows, LANES), 8)
        for d in range(2):
            turned_ref[d, :, : 2 * rows] = jnp.transpose(theirs_ref[j, d])
            mine = turned_ref[d, pl.ds(offset, rows), : 2 * rows]
            hi, lo = split_bf16(jnp.where(live_in & live_out, SECTION_STEP * mine, 0.0))
            wsend_ref[j, d * rows : (d + 1) * rows] = jnp.concatenate([hi, lo, hi], axis=1)


def own_kernel(
    owner_ref,
    rows_ref,
    coef_ref,
    wown_ref,
    q_ref,
    tile_ref,
    dx_ref,
    dxx_ref,
    out_ref,
    hi_ref,
    lo_ref,
):
    nvar, rows, _ = q_ref.shape[1:]
    live_rows = rows_ref[find_block(owner_ref, lax.axis_index("blk"))]

    @pl.when(pl.program_id(0) == 0)
    def _():
        for v in range(nvar):
            hi, lo = split_bf16(q_ref[0, v])
            hi_ref[v * rows : (v + 1) * rows] = hi
            lo_ref[v * rows : (v + 1) * rows] = lo

    def derivative(op_ref):
        hi, lo = split_bf16(op_ref[...])
        return dot(hi_ref[...], hi) + dot(lo_ref[...], hi) + dot(hi_ref[...], lo)

    dx = derivative(dx_ref)
    dxx = derivative(dxx_ref)
    u, w = tile_ref[0, 0], tile_ref[0, 1]
    live = lax.axis_index("line") * rows + lax.broadcasted_iota(jnp.int32, u.shape, 0) < live_rows
    for v in range(nvar):
        here = slice(v * rows, (v + 1) * rows)
        dy = dot(wown_ref[...], three_parts([tile_ref[0, v]]))
        rhs = coef_ref[v] * dxx[here] - u * dx[here]
        if v == 1:
            rhs = rhs + coef_ref[nvar] * tile_ref[0, 3] + coef_ref[nvar + 1] * tile_ref[0, 4]
        value = jnp.where(live, tile_ref[0, v] + SECTION_STEP * rhs, 0.0)
        out_ref[0, v] = value + coef_ref[v] * dy[rows:] - w * dy[:rows]


def near_kernel(
    face_count,
    owner_ref,
    link_ref,
    side_ref,
    rows_ref,
    gop_ref,
    wnear_ref,
    nu_ref,
    q_ref,
    base_ref,
    near_raw_ref,
    *refs,
):
    near_sent, refs = refs[0], refs[1:]
    faces, (out_ref,) = refs[:face_count], refs[face_count:]
    near = {v: near_sent.at[0, i] for i, v in enumerate(SENT)}
    near.update({v: near_raw_ref.at[0, i] for i, v in enumerate(RAW)})
    nvar, rows, x_length = q_ref.shape[1:]
    my_slot = lax.axis_index("blk")
    my_block = find_block(owner_ref, my_slot)
    sides = [side_ref[m, my_block] for m in range(2)]
    live_rows = rows_ref[my_block]
    y_index = lax.axis_index("line") * rows + lax.broadcasted_iota(jnp.int32, (FACE_ROWS, rows), 1)
    scale = jnp.where(y_index < live_rows, SECTION_STEP, 0.0)

    planes = []
    for m in range(2):
        place = jnp.bitwise_xor(owner_ref[link_ref[m, my_block]], my_slot)
        plane, first = faces[0][0, sides[m]], 1
        for ref in faces[1:]:
            count = ref.shape[0]
            at = jnp.clip(place - first, 0, count - 1)
            plane = jnp.where(place >= first, ref[at, sides[m]], plane)
            first += count
        planes.append(plane * scale)

    def ghost_rows(g):
        parts = []
        for m in range(2):
            straight = g[GHOST * m : GHOST * (m + 1)]
            turned = jnp.concatenate([straight[2:3], straight[1:2], straight[0:1]], axis=0)
            parts.append(jnp.where(sides[m] == m, turned, straight))
        hi, lo = split_bf16(jnp.concatenate(parts, axis=0))
        pad = jnp.zeros((LANES - 6 * GHOST, hi.shape[1]), jnp.float32)
        stacked = [hi.astype(jnp.float32), hi.astype(jnp.float32), lo.astype(jnp.float32)]
        return jnp.concatenate(stacked + [pad], axis=0).astype(jnp.bfloat16)

    operator = ghost_rows(gop_ref[...])
    pad = jnp.zeros((LANES - 6 * GHOST, rows), jnp.float32)
    for v in range(nvar):
        parts = []
        for m in range(2):
            part = planes[m][GHOST * v : GHOST * (v + 1)]
            if v == 0:
                part = jnp.where(sides[m] == m, -part, part)
            parts.append(part)
        hi, lo = split_bf16(jnp.concatenate(parts, axis=0))
        stacked = [hi.astype(jnp.float32), lo.astype(jnp.float32), hi.astype(jnp.float32)]
        ghost = jnp.transpose(jnp.concatenate(stacked + [pad], axis=0)).astype(jnp.bfloat16)
        dx = dot(ghost, operator)
        dy = dot(wnear_ref[...], three_parts([near[v][...]]))
        second = nu_ref[v, 0:1] * (dx[:, x_length:] + dy[rows:])
        out_ref[0, v] = base_ref[0, v] + second - q_ref[0, 0] * dx[:, :x_length] - q_ref[0, 1] * dy[:rows]


def send_kernel(wsend_ref, nu_ref, q_ref, *refs):
    count = wsend_ref.shape[0]
    far_v, near, out = refs[:count], refs[count], refs[count + 1 :]
    rows = q_ref.shape[2]
    for j in range(count):
        for i, v in enumerate(SENT):
            dy = dot(wsend_ref[j], three_parts([q_ref[0, v], near[0, i]]))
            out[j][0, i] = nu_ref[v, 0:1] * dy[rows:] - far_v[j][0, 0] * dy[:rows]


def raw_kernel(count, wdirect_ref, wpassed_ref, nu_ref, q_ref, base_ref, *refs):
    *refs, out_ref, done_ref, sems = refs
    rows = q_ref.shape[2]
    copies = []
    for low, high in (FIRST, SECOND):
        direct, refs = refs[:count], refs[count:]
        for v in range(low, high):
            i = v - RAW[0]
            passed, refs = refs[:count], refs[count:]
            dy = dot(wdirect_ref[...], three_parts([piece[0, v - low] for piece in direct]))
            dy = dy + dot(wpassed_ref[...], three_parts([piece[0, 0] for piece in passed]))
            done_ref[i] = base_ref[0, v] + nu_ref[v, 0:1] * dy[rows:] - q_ref[0, 1] * dy[:rows]
            copies.append(pltpu.make_async_copy(done_ref.at[i], out_ref.at[0, v], sems.at[i]))
            copies[-1].start()
    for copy in copies:
        copy.wait()


def last_kernel(base_ref, *refs):
    results, (_, out_ref, done_ref, sems) = refs[:-4], refs[-4:]
    copies = []
    for i, v in enumerate(SENT):
        done_ref[i] = base_ref[0, v] + sum(piece[0, i] for piece in results)
        copies.append(pltpu.make_async_copy(done_ref.at[i], out_ref.at[0, v], sems.at[i]))
        copies[-1].start()
    for copy in copies:
        copy.wait()


def smem():
    return pl.BlockSpec(memory_space=SMEM)


def kept():
    return pl.BlockSpec(memory_space=VMEM)


def held(array):
    return pltpu.with_memory_space_constraint(array, VMEM)


def on_device(
    slots,
    lines,
    flow_state,
    block_owner,
    link_block,
    link_side,
    rows_live,
    x_operator,
    ghost_operator,
    y_operator,
    coefficients,
):
    _, nvar, rows, x_length = flow_state.shape
    y_length = lines * rows
    limit = pltpu.CompilerParams(vmem_limit_bytes=16 * 1024 * 1024)
    small = pl.CostEstimate(flops=1, bytes_accessed=1, transcendentals=0)
    state_shape = jax.ShapeDtypeStruct(flow_state.shape, jnp.float32)
    sibling = [(i, i ^ 1) for i in range(lines)]
    shifts = range(2, lines, 2)

    def across(array):
        return [lax.ppermute(array, "line", [(i, (i + s) % lines) for i in range(lines)]) for s in shifts]

    low, high = FIRST
    part = pl.pallas_call(
        functools.partial(part_kernel, low),
        in_specs=[pl.BlockSpec(memory_space=pl.ANY)],
        out_specs=pl.BlockSpec(memory_space=VMEM),
        out_shape=jax.ShapeDtypeStruct((1, high - low, rows, x_length), jnp.float32),
        scratch_shapes=[pltpu.SemaphoreType.DMA],
        compiler_params=limit,
        cost_estimate=small,
        name="part",
    )(pltpu.with_memory_space_constraint(flow_state, HBM))
    direct_first = across(part)

    in_hbm = pltpu.with_memory_space_constraint(flow_state, HBM)
    flow_state, faces = pl.pallas_call(
        faces_kernel,
        in_specs=[smem(), smem(), kept(), pl.BlockSpec(memory_space=pl.ANY)],
        out_specs=[kept(), kept()],
        out_shape=[state_shape, jax.ShapeDtypeStruct((1, 2, FACE_ROWS, rows), jnp.float32)],
        scratch_shapes=[pltpu.SemaphoreType.DMA((nvar,))],
        compiler_params=limit,
        cost_estimate=small,
        name="faces",
    )(block_owner, rows_live, held(part), in_hbm)
    second = flow_state[:, SECOND[0] : SECOND[1]]
    direct_second = across(second)
    near_sent = lax.ppermute(
        jnp.concatenate([flow_state[:, v : v + 1] for v in SENT], axis=1), "line", sibling
    )

    w_near = jax.ShapeDtypeStruct((2 * rows, 3 * rows), jnp.bfloat16)
    w_far = jax.ShapeDtypeStruct((2 * rows, 3 * len(shifts) * rows), jnp.bfloat16)
    w_send = jax.ShapeDtypeStruct((len(shifts), 2 * rows, 6 * rows), jnp.bfloat16)
    nu = jax.ShapeDtypeStruct((nvar, 8, x_length), jnp.float32)
    w_own, w_near, w_direct, w_passed, w_send, nu = pl.pallas_call(
        functools.partial(weights_kernel, lines),
        in_specs=[smem()] * 3 + [pl.BlockSpec(memory_space=pl.ANY)],
        out_specs=[kept()] * 6,
        out_shape=[w_near, w_near, w_far, w_far, w_send, nu],
        scratch_shapes=[
            pltpu.VMEM((2, y_length, LANES), jnp.float32),
            pltpu.VMEM((2, LANES, y_length), jnp.float32),
            pltpu.VMEM((len(shifts), 2, 2 * rows, LANES), jnp.float32),
            pltpu.VMEM((lines, 2 * rows, rows), jnp.bfloat16),
            pltpu.VMEM((lines, 2 * rows, rows), jnp.bfloat16),
            pltpu.SemaphoreType.DMA((2 + 4 * len(shifts),)),
        ],
        compiler_params=limit,
        cost_estimate=small,
        name="weights",
    )(block_owner, rows_live, coefficients, pltpu.with_memory_space_constraint(y_operator, HBM))

    tiles = x_length // TILE
    def own_terms(w_own):
        return pl.pallas_call(
            own_kernel,
            grid=(tiles,),
            in_specs=[smem()] * 3
            + [
                pl.BlockSpec(w_own.shape, lambda n: (0, 0)),
                pl.BlockSpec((1, nvar, rows, x_length), lambda n: (0, 0, 0, 0)),
                pl.BlockSpec((1, nvar, rows, TILE), lambda n: (0, 0, 0, n)),
                pl.BlockSpec((x_length, TILE), lambda n: (0, n)),
                pl.BlockSpec((x_length, TILE), lambda n: (0, n + tiles)),
            ],
            out_specs=pl.BlockSpec((1, nvar, rows, TILE), lambda n: (0, 0, 0, n)),
            out_shape=state_shape,
            scratch_shapes=[
                pltpu.VMEM((nvar * rows, x_length), jnp.bfloat16),
                pltpu.VMEM((nvar * rows, x_length), jnp.bfloat16),
            ],
            compiler_params=limit,
            cost_estimate=small,
            name="own_terms",
        )(
            block_owner,
            rows_live,
            coefficients,
            w_own,
            flow_state,
            flow_state,
            *[pltpu.with_memory_space_constraint(x_operator, HBM)] * 2,
        )

    far_v = [direct_first[shifts.index(lines - s)] for s in shifts]
    sent = jax.ShapeDtypeStruct((1, len(SENT), rows, x_length), jnp.float32)
    send = pl.pallas_call(
        send_kernel,
        in_specs=[kept()] * (4 + len(shifts)),
        out_specs=[kept()] * len(shifts),
        out_shape=[sent] * len(shifts),
        compiler_params=limit,
        cost_estimate=small,
        name="send_terms",
    )
    arrived = [faces]
    held_faces, step = faces, 1
    while step < slots:
        there = lax.ppermute(held_faces, "blk", [(i, i ^ step) for i in range(slots)])
        if step == 1:
            there, w_own, own = lax.optimization_barrier((there, w_own, flow_state))
            near_raw = lax.ppermute(own[:, RAW[0] : RAW[-1] + 1], "line", sibling)
        elif step == 2:
            w_send, *_ = lax.optimization_barrier((w_send, there))
            results = send(*map(held, (w_send, nu, flow_state, *far_v, near_sent)))
            direct_first, *_ = lax.optimization_barrier((direct_first, *results))
            w_own, *_ = lax.optimization_barrier((w_own, *results))
            state = own_terms(w_own)
        arrived.append(there)
        step *= 2
        if step < slots:
            held_faces = jnp.concatenate([held_faces, there], axis=0)

    results = [
        lax.ppermute(result, "line", [(i, (i + s) % lines) for i in range(lines)])
        for s, result in zip(shifts, results)
    ]

    passed_first = [
        lax.ppermute(piece[:, i : i + 1], "line", sibling)
        for i in range(FIRST[1] - FIRST[0])
        for piece in direct_first
    ]
    direct_second, *_ = lax.optimization_barrier((direct_second, state, *arrived))
    passed_second = [lax.ppermute(piece, "line", sibling) for piece in direct_second]
    pieces = [*direct_first, *passed_first, *direct_second, *passed_second]

    state = pl.pallas_call(
        functools.partial(near_kernel, len(arrived)),
        in_specs=[smem()] * 4 + [kept()] * (7 + len(arrived)),
        out_specs=kept(),
        out_shape=state_shape,
        compiler_params=limit,
        cost_estimate=small,
        name="near_terms",
    )(
        block_owner,
        link_block.T,
        link_side.T,
        rows_live,
        *map(held, (ghost_operator, w_near, nu, flow_state, state, near_raw, near_sent, *arrived)),
    )

    anywhere = pl.BlockSpec(memory_space=pl.ANY)
    result = pl.pallas_call(
        functools.partial(raw_kernel, len(shifts)),
        in_specs=[kept()] * (5 + len(pieces)),
        out_specs=anywhere,
        out_shape=state_shape,
        scratch_shapes=[
            pltpu.VMEM((len(RAW), rows, x_length), jnp.float32),
            pltpu.SemaphoreType.DMA((len(RAW),)),
        ],
        compiler_params=limit,
        cost_estimate=small,
        name="raw_terms",
    )(*map(held, (w_direct, w_passed, nu, flow_state, state, *pieces)))

    operands = [*map(held, (state, *results))]
    return pl.pallas_call(
        last_kernel,
        in_specs=[kept()] * len(operands) + [anywhere],
        out_specs=anywhere,
        out_shape=state_shape,
        input_output_aliases={len(operands): 0},
        scratch_shapes=[pltpu.VMEM(sent.shape[1:], jnp.float32), pltpu.SemaphoreType.DMA((len(SENT),))],
        compiler_params=limit,
        cost_estimate=small,
        name="last_terms",
    )(*operands, result)


def solution(mesh):
    return jax.shard_map(
        functools.partial(on_device, mesh.shape["blk"], mesh.shape["line"]),
        mesh=mesh,
        in_specs=(P("blk", None, "line", None), P(), P(), P(), P(), P(), P(), P(), P()),
        out_specs=P("blk", None, "line", None),
        check_vma=False,
    )
```

```python
import functools

import jax
import jax.numpy as jnp
from jax import lax
from jax.experimental import pallas as pl
from jax.experimental.pallas import tpu as pltpu
from jax.sharding import PartitionSpec as P

GHOST = 3
SECTION_STEP = 0.3
FACE_ROWS = 16
TILE = 256
LANES = 128
FIRST, SECOND = (1, 3), (3, 4)
RAW = tuple(range(FIRST[0], SECOND[1]))
SENT = (0, 4)

SMEM = pltpu.MemorySpace.SMEM
VMEM = pltpu.MemorySpace.VMEM
HBM = pltpu.MemorySpace.HBM


def split_bf16(x):
    hi = x.astype(jnp.bfloat16)
    lo = (x - hi.astype(jnp.float32)).astype(jnp.bfloat16)
    return hi, lo


def dot(a, b):
    return jnp.dot(a, b, preferred_element_type=jnp.float32)


def three_parts(pieces):
    split = [split_bf16(piece) for piece in pieces]
    hi = [s[0] for s in split]
    lo = [s[1] for s in split]
    return jnp.concatenate(hi + hi + lo, axis=0)


def find_block(owner_ref, my_slot):
    return lax.fori_loop(
        0, owner_ref.shape[0], lambda i, found: jnp.where(owner_ref[i] == my_slot, i, found), 0
    )


def faces_kernel(owner_ref, rows_ref, part_ref, q_ref, held_ref, out_ref, sems):
    nvar, rows, x_length = held_ref.shape[1:]
    copies = [pltpu.make_async_copy(q_ref.at[0, v], held_ref.at[0, v], sems.at[v]) for v in range(nvar)]
    for copy in copies:
        copy.start()
    live_rows = rows_ref[find_block(owner_ref, lax.axis_index("blk"))]
    y_index = lax.axis_index("line") * rows + lax.broadcasted_iota(jnp.int32, (GHOST, rows), 1)
    live = y_index < live_rows
    for m in range(2):
        out_ref[0, m, GHOST * nvar :, :] = jnp.zeros((FACE_ROWS - GHOST * nvar, rows), jnp.float32)
    for v in range(nvar):
        copies[v].wait()
        low = jnp.transpose(held_ref[0, v, :, :LANES])[:GHOST]
        high = jnp.transpose(held_ref[0, v, :, x_length - LANES :])[LANES - GHOST :]
        out_ref[0, 0, GHOST * v : GHOST * (v + 1), :] = jnp.where(live, low, 0.0)
        out_ref[0, 1, GHOST * v : GHOST * (v + 1), :] = jnp.where(live, high, 0.0)


def part_kernel(low, q_ref, out_ref, sem):
    copy = pltpu.make_async_copy(q_ref.at[:, low : low + out_ref.shape[1]], out_ref, sem)
    copy.start()
    copy.wait()


def weights_kernel(
    lines,
    owner_ref,
    rows_ref,
    coef_ref,
    yop_ref,
    wown_ref,
    wnear_ref,
    wdirect_ref,
    wsibling_ref,
    wsend_ref,
    nu_ref,
    columns_ref,
    turned_ref,
    theirs_ref,
    pieces_hi_ref,
    pieces_lo_ref,
    sems,
):
    y_length = yop_ref.shape[0]
    rows = y_length // lines
    line_pos = lax.axis_index("line")
    other = jnp.bitwise_xor(line_pos, 1)
    shifts = range(2, lines, 2)
    targets = [lax.rem(line_pos + s, lines) for s in shifts]

    def column(d, line):
        return pl.ds(pl.multiple_of(d * y_length + (line * rows) // LANES * LANES, LANES), LANES)

    copies = []
    for d in range(2):
        source = yop_ref.at[:, column(d, line_pos)]
        copies.append(pltpu.make_async_copy(source, columns_ref.at[d], sems.at[d]))
    direct = [lax.rem(line_pos + lines - s, lines) for s in shifts]
    others = [(target, [line_pos, other]) for target in targets] + [(other, [line_pos] + direct)]
    for j, (target, sources) in enumerate(others):
        for d in range(2):
            for i, line in enumerate(sources):
                source = yop_ref.at[pl.ds(pl.multiple_of(line * rows, 8), rows), column(d, target)]
                goal = theirs_ref.at[j, d, i * rows : (i + 1) * rows]
                copies.append(pltpu.make_async_copy(source, goal, sems.at[len(copies)]))
    for copy in copies:
        copy.start()

    live_rows = rows_ref[find_block(owner_ref, lax.axis_index("blk"))]
    for v in range(nu_ref.shape[0]):
        nu_ref[v] = jnp.full(nu_ref.shape[1:], coef_ref[v], jnp.float32)
    for copy in copies:
        copy.wait()

    shape = (rows, y_length)
    live_in = lax.broadcasted_iota(jnp.int32, shape, 1) < live_rows
    live_out = line_pos * rows + lax.broadcasted_iota(jnp.int32, shape, 0) < live_rows
    offset = pl.multiple_of(lax.rem(line_pos * rows, LANES), 8)
    for d in range(2):
        turned_ref[d] = jnp.transpose(columns_ref[d])
        mine = turned_ref[d, pl.ds(offset, rows), :]
        hi, lo = split_bf16(jnp.where(live_in & live_out, SECTION_STEP * mine, 0.0))
        for p in range(lines):
            pieces_hi_ref[p, d * rows : (d + 1) * rows] = hi[:, p * rows : (p + 1) * rows]
            pieces_lo_ref[p, d * rows : (d + 1) * rows] = lo[:, p * rows : (p + 1) * rows]

    def gather(ref, places):
        hi = [pieces_hi_ref[p] for p in places]
        lo = [pieces_lo_ref[p] for p in places]
        ref[...] = jnp.concatenate(hi + lo + hi, axis=1)

    gather(wown_ref, [line_pos])
    gather(wnear_ref, [other])
    gather(wdirect_ref, direct)

    for j, (target, sources) in enumerate(others):
        depth = len(sources) * rows
        shape = (rows, rows)
        ins = [line * rows + lax.broadcasted_iota(jnp.int32, shape, 1) for line in sources]
        live_in = jnp.concatenate(ins, axis=1) < live_rows
        live_out = target * rows + lax.broadcasted_iota(jnp.int32, live_in.shape, 0) < live_rows
        offset = pl.multiple_of(lax.rem(target * rows, LANES), 8)
        goal = wsend_ref.at[j] if j < len(targets) else wsibling_ref
        for d in range(2):
            turned_ref[d, :, :depth] = jnp.transpose(theirs_ref[j, d, :depth])
            mine = turned_ref[d, pl.ds(offset, rows), :depth]
            hi, lo = split_bf16(jnp.where(live_in & live_out, SECTION_STEP * mine, 0.0))
            goal[d * rows : (d + 1) * rows] = jnp.concatenate([hi, lo, hi], axis=1)


def own_kernel(
    owner_ref,
    rows_ref,
    coef_ref,
    wown_ref,
    q_ref,
    tile_ref,
    dx_ref,
    dxx_ref,
    out_ref,
    hi_ref,
    lo_ref,
):
    nvar, rows, _ = q_ref.shape[1:]
    live_rows = rows_ref[find_block(owner_ref, lax.axis_index("blk"))]

    @pl.when(pl.program_id(0) == 0)
    def _():
        for v in range(nvar):
            hi, lo = split_bf16(q_ref[0, v])
            hi_ref[v * rows : (v + 1) * rows] = hi
            lo_ref[v * rows : (v + 1) * rows] = lo

    def derivative(op_ref):
        hi, lo = split_bf16(op_ref[...])
        return dot(hi_ref[...], hi) + dot(lo_ref[...], hi) + dot(hi_ref[...], lo)

    dx = derivative(dx_ref)
    dxx = derivative(dxx_ref)
    u, w = tile_ref[0, 0], tile_ref[0, 1]
    live = lax.axis_index("line") * rows + lax.broadcasted_iota(jnp.int32, u.shape, 0) < live_rows
    for v in range(nvar):
        here = slice(v * rows, (v + 1) * rows)
        dy = dot(wown_ref[...], three_parts([tile_ref[0, v]]))
        rhs = coef_ref[v] * dxx[here] - u * dx[here]
        if v == 1:
            rhs = rhs + coef_ref[nvar] * tile_ref[0, 3] + coef_ref[nvar + 1] * tile_ref[0, 4]
        value = jnp.where(live, tile_ref[0, v] + SECTION_STEP * rhs, 0.0)
        out_ref[0, v] = value + coef_ref[v] * dy[rows:] - w * dy[:rows]


def near_kernel(
    face_count,
    owner_ref,
    link_ref,
    side_ref,
    rows_ref,
    gop_ref,
    wnear_ref,
    wdirect_ref,
    nu_ref,
    q_ref,
    base_ref,
    near_ref,
    *refs,
):
    faces, refs = refs[:face_count], refs[face_count:]
    *refs, out_ref, left_ref, done_ref, sems = refs
    count = (len(refs) - len(RAW)) // 2
    raw = {}
    for low, high in (FIRST, SECOND):
        direct, refs = refs[:count], refs[count:]
        for v in range(low, high):
            raw[v] = [ref.at[0, v - low] for ref in direct] + [refs[v - low].at[0, 0]]
        refs = refs[high - low :]
    nvar, rows, x_length = q_ref.shape[1:]
    my_slot = lax.axis_index("blk")
    my_block = find_block(owner_ref, my_slot)
    sides = [side_ref[m, my_block] for m in range(2)]
    live_rows = rows_ref[my_block]
    y_index = lax.axis_index("line") * rows + lax.broadcasted_iota(jnp.int32, (FACE_ROWS, rows), 1)
    scale = jnp.where(y_index < live_rows, SECTION_STEP, 0.0)

    planes = []
    for m in range(2):
        place = jnp.bitwise_xor(owner_ref[link_ref[m, my_block]], my_slot)
        plane, first = faces[0][0, sides[m]], 1
        for ref in faces[1:]:
            count = ref.shape[0]
            at = jnp.clip(place - first, 0, count - 1)
            plane = jnp.where(place >= first, ref[at, sides[m]], plane)
            first += count
        planes.append(plane * scale)

    def ghost_rows(g):
        parts = []
        for m in range(2):
            straight = g[GHOST * m : GHOST * (m + 1)]
            turned = jnp.concatenate([straight[2:3], straight[1:2], straight[0:1]], axis=0)
            parts.append(jnp.where(sides[m] == m, turned, straight))
        hi, lo = split_bf16(jnp.concatenate(parts, axis=0))
        pad = jnp.zeros((LANES - 6 * GHOST, hi.shape[1]), jnp.float32)
        stacked = [hi.astype(jnp.float32), hi.astype(jnp.float32), lo.astype(jnp.float32)]
        return jnp.concatenate(stacked + [pad], axis=0).astype(jnp.bfloat16)

    operator = ghost_rows(gop_ref[...])
    pad = jnp.zeros((LANES - 6 * GHOST, rows), jnp.float32)
    copies = []
    for v in RAW + SENT:
        parts = []
        for m in range(2):
            part = planes[m][GHOST * v : GHOST * (v + 1)]
            if v == 0:
                part = jnp.where(sides[m] == m, -part, part)
            parts.append(part)
        hi, lo = split_bf16(jnp.concatenate(parts, axis=0))
        stacked = [hi.astype(jnp.float32), lo.astype(jnp.float32), hi.astype(jnp.float32)]
        ghost = jnp.transpose(jnp.concatenate(stacked + [pad], axis=0)).astype(jnp.bfloat16)
        dx = dot(ghost, operator)
        if v in SENT:
            dy = dot(wnear_ref[...], three_parts([near_ref[0, SENT.index(v)]]))
        else:
            *direct, from_sibling = raw[v]
            dy = dot(wdirect_ref[...], three_parts([ref[...] for ref in direct]))
        second = nu_ref[v, 0:1] * (dx[:, x_length:] + dy[rows:])
        value = base_ref[0, v] + second - q_ref[0, 0] * dx[:, :x_length] - q_ref[0, 1] * dy[:rows]
        if v in SENT:
            left_ref[0, SENT.index(v)] = value
            continue
        i = RAW.index(v)
        done_ref[i] = value + from_sibling[...]
        copies.append(pltpu.make_async_copy(done_ref.at[i], out_ref.at[0, v], sems.at[i]))
        copies[-1].start()
    for copy in copies:
        copy.wait()


def send_kernel(wsend_ref, nu_ref, q_ref, *refs):
    count = wsend_ref.shape[0]
    far_v, near, out = refs[:count], refs[count], refs[count + 1 :]
    rows = q_ref.shape[2]
    for j in range(count):
        for i, v in enumerate(SENT):
            dy = dot(wsend_ref[j], three_parts([q_ref[0, v], near[0, i]]))
            out[j][0, i] = nu_ref[v, 0:1] * dy[rows:] - far_v[j][0, 0] * dy[:rows]


def sibling_kernel(low, high, w_ref, nu_ref, q_ref, near_v_ref, *refs):
    direct, out = refs[: low - high], refs[low - high :]
    rows = q_ref.shape[2]
    for i in range(high - low):
        v = low + i
        dy = dot(w_ref[...], three_parts([q_ref[0, v]] + [piece[0, i] for piece in direct]))
        out[i][0, 0] = nu_ref[v, 0:1] * dy[rows:] - near_v_ref[0, 0] * dy[:rows]


def last_kernel(left_ref, *refs):
    results, (_, out_ref, done_ref, sems) = refs[:-4], refs[-4:]
    copies = []
    for i, v in enumerate(SENT):
        done_ref[i] = left_ref[0, i] + sum(piece[0, i] for piece in results)
        copies.append(pltpu.make_async_copy(done_ref.at[i], out_ref.at[0, v], sems.at[i]))
        copies[-1].start()
    for copy in copies:
        copy.wait()


def smem():
    return pl.BlockSpec(memory_space=SMEM)


def kept():
    return pl.BlockSpec(memory_space=VMEM)


def held(array):
    return pltpu.with_memory_space_constraint(array, VMEM)


def on_device(
    slots,
    lines,
    flow_state,
    block_owner,
    link_block,
    link_side,
    rows_live,
    x_operator,
    ghost_operator,
    y_operator,
    coefficients,
):
    _, nvar, rows, x_length = flow_state.shape
    y_length = lines * rows
    limit = pltpu.CompilerParams(vmem_limit_bytes=16 * 1024 * 1024)
    small = pl.CostEstimate(flops=1, bytes_accessed=1, transcendentals=0)
    state_shape = jax.ShapeDtypeStruct(flow_state.shape, jnp.float32)
    sibling = [(i, i ^ 1) for i in range(lines)]
    shifts = range(2, lines, 2)

    def across(array):
        return [lax.ppermute(array, "line", [(i, (i + s) % lines) for i in range(lines)]) for s in shifts]

    low, high = FIRST
    part = pl.pallas_call(
        functools.partial(part_kernel, low),
        in_specs=[pl.BlockSpec(memory_space=pl.ANY)],
        out_specs=pl.BlockSpec(memory_space=VMEM),
        out_shape=jax.ShapeDtypeStruct((1, high - low, rows, x_length), jnp.float32),
        scratch_shapes=[pltpu.SemaphoreType.DMA],
        compiler_params=limit,
        cost_estimate=small,
        name="part",
    )(pltpu.with_memory_space_constraint(flow_state, HBM))
    direct_first = across(part)

    in_hbm = pltpu.with_memory_space_constraint(flow_state, HBM)
    flow_state, faces = pl.pallas_call(
        faces_kernel,
        in_specs=[smem(), smem(), kept(), pl.BlockSpec(memory_space=pl.ANY)],
        out_specs=[kept(), kept()],
        out_shape=[state_shape, jax.ShapeDtypeStruct((1, 2, FACE_ROWS, rows), jnp.float32)],
        scratch_shapes=[pltpu.SemaphoreType.DMA((nvar,))],
        compiler_params=limit,
        cost_estimate=small,
        name="faces",
    )(block_owner, rows_live, held(part), in_hbm)
    second = flow_state[:, SECOND[0] : SECOND[1]]
    direct_second = across(second)
    near = lax.ppermute(
        jnp.concatenate([flow_state[:, v : v + 1] for v in SENT], axis=1), "line", sibling
    )

    w_near = jax.ShapeDtypeStruct((2 * rows, 3 * rows), jnp.bfloat16)
    w_far = jax.ShapeDtypeStruct((2 * rows, 3 * len(shifts) * rows), jnp.bfloat16)
    w_sibling = jax.ShapeDtypeStruct((2 * rows, 3 * (1 + len(shifts)) * rows), jnp.bfloat16)
    w_send = jax.ShapeDtypeStruct((len(shifts), 2 * rows, 6 * rows), jnp.bfloat16)
    nu = jax.ShapeDtypeStruct((nvar, 8, x_length), jnp.float32)
    w_own, w_near, w_direct, w_sibling, w_send, nu = pl.pallas_call(
        functools.partial(weights_kernel, lines),
        in_specs=[smem()] * 3 + [pl.BlockSpec(memory_space=pl.ANY)],
        out_specs=[kept()] * 6,
        out_shape=[w_near, w_near, w_far, w_sibling, w_send, nu],
        scratch_shapes=[
            pltpu.VMEM((2, y_length, LANES), jnp.float32),
            pltpu.VMEM((2, LANES, y_length), jnp.float32),
            pltpu.VMEM((len(shifts) + 1, 2, max(2, lines // 2) * rows, LANES), jnp.float32),
            pltpu.VMEM((lines, 2 * rows, rows), jnp.bfloat16),
            pltpu.VMEM((lines, 2 * rows, rows), jnp.bfloat16),
            pltpu.SemaphoreType.DMA((2 + 4 * len(shifts) + lines,)),
        ],
        compiler_params=limit,
        cost_estimate=small,
        name="weights",
    )(block_owner, rows_live, coefficients, pltpu.with_memory_space_constraint(y_operator, HBM))

    tiles = x_length // TILE
    def own_terms(w_own):
        return pl.pallas_call(
            own_kernel,
            grid=(tiles,),
            in_specs=[smem()] * 3
            + [
                pl.BlockSpec(w_own.shape, lambda n: (0, 0)),
                pl.BlockSpec((1, nvar, rows, x_length), lambda n: (0, 0, 0, 0)),
                pl.BlockSpec((1, nvar, rows, TILE), lambda n: (0, 0, 0, n)),
                pl.BlockSpec((x_length, TILE), lambda n: (0, n)),
                pl.BlockSpec((x_length, TILE), lambda n: (0, n + tiles)),
            ],
            out_specs=pl.BlockSpec((1, nvar, rows, TILE), lambda n: (0, 0, 0, n)),
            out_shape=state_shape,
            scratch_shapes=[
                pltpu.VMEM((nvar * rows, x_length), jnp.bfloat16),
                pltpu.VMEM((nvar * rows, x_length), jnp.bfloat16),
            ],
            compiler_params=limit,
            cost_estimate=small,
            name="own_terms",
        )(
            block_owner,
            rows_live,
            coefficients,
            w_own,
            flow_state,
            flow_state,
            *[pltpu.with_memory_space_constraint(x_operator, HBM)] * 2,
        )

    far_v = [direct_first[shifts.index(lines - s)] for s in shifts]
    sent = jax.ShapeDtypeStruct((1, len(SENT), rows, x_length), jnp.float32)
    send = pl.pallas_call(
        send_kernel,
        in_specs=[kept()] * (4 + len(shifts)),
        out_specs=[kept()] * len(shifts),
        out_shape=[sent] * len(shifts),
        compiler_params=limit,
        cost_estimate=small,
        name="send_terms",
    )
    arrived = [faces]
    held_faces, step = faces, 1
    while step < slots:
        there = lax.ppermute(held_faces, "blk", [(i, i ^ step) for i in range(slots)])
        if step == 1:
            there, w_own, own = lax.optimization_barrier((there, w_own, flow_state))
            near_v = lax.ppermute(own[:, 1:2], "line", sibling)
        elif step == 2:
            state = own_terms(w_own)
            w_send, *_ = lax.optimization_barrier((w_send, state, there))
            results = send(*map(held, (w_send, nu, flow_state, *far_v, near)))
            direct_first, *_ = lax.optimization_barrier((direct_first, *results))
            direct_second, *_ = lax.optimization_barrier((direct_second, *results))
        arrived.append(there)
        step *= 2
        if step < slots:
            held_faces = jnp.concatenate([held_faces, there], axis=0)

    results = [
        lax.ppermute(result, "line", [(i, (i + s) % lines) for i in range(lines)])
        for s, result in zip(shifts, results)
    ]

    def sibling_terms(part, direct):
        operands = [*map(held, (w_sibling, nu, flow_state, near_v, *direct))]
        low, high = part
        results = pl.pallas_call(
            functools.partial(sibling_kernel, low, high),
            in_specs=[kept()] * len(operands),
            out_specs=[kept()] * (high - low),
            out_shape=[jax.ShapeDtypeStruct((1, 1, rows, x_length), jnp.float32)] * (high - low),
            compiler_params=limit,
            cost_estimate=small,
            name="sibling_terms",
        )(*operands)
        return [*direct, *(lax.ppermute(result, "line", sibling) for result in results)]

    direct_second, *_ = lax.optimization_barrier((direct_second, *arrived))
    pieces = sibling_terms(FIRST, direct_first) + sibling_terms(SECOND, direct_second)

    anywhere = pl.BlockSpec(memory_space=pl.ANY)
    result, left = pl.pallas_call(
        functools.partial(near_kernel, len(arrived)),
        in_specs=[smem()] * 4 + [kept()] * (7 + len(arrived) + len(pieces)),
        out_specs=[anywhere, kept()],
        out_shape=[state_shape, sent],
        scratch_shapes=[
            pltpu.VMEM((len(RAW), rows, x_length), jnp.float32),
            pltpu.SemaphoreType.DMA((len(RAW),)),
        ],
        compiler_params=limit,
        cost_estimate=small,
        name="near_terms",
    )(
        block_owner,
        link_block.T,
        link_side.T,
        rows_live,
        *map(held, (ghost_operator, w_near, w_direct, nu, flow_state, state, near, *arrived, *pieces)),
    )

    operands = [*map(held, (left, *results))]
    return pl.pallas_call(
        last_kernel,
        in_specs=[kept()] * len(operands) + [anywhere],
        out_specs=anywhere,
        out_shape=state_shape,
        input_output_aliases={len(operands): 0},
        scratch_shapes=[pltpu.VMEM(sent.shape[1:], jnp.float32), pltpu.SemaphoreType.DMA((len(SENT),))],
        compiler_params=limit,
        cost_estimate=small,
        name="last_terms",
    )(*operands, result)


def solution(mesh):
    return jax.shard_map(
        functools.partial(on_device, mesh.shape["blk"], mesh.shape["line"]),
        mesh=mesh,
        in_specs=(P("blk", None, "line", None), P(), P(), P(), P(), P(), P(), P(), P()),
        out_specs=P("blk", None, "line", None),
        check_vma=False,
    )
```

```python
import functools

import jax
import jax.numpy as jnp
from jax import lax
from jax.experimental import pallas as pl
from jax.experimental.pallas import tpu as pltpu
from jax.sharding import PartitionSpec as P

GHOST = 3
SECTION_STEP = 0.3
FACE_ROWS = 16
TILE = 256
LANES = 128
FIRST, SECOND = (1, 2), (2, 4)
RAW = tuple(range(FIRST[0], SECOND[1]))
SENT = (0, 4)

SMEM = pltpu.MemorySpace.SMEM
VMEM = pltpu.MemorySpace.VMEM
HBM = pltpu.MemorySpace.HBM


def split_bf16(x):
    hi = x.astype(jnp.bfloat16)
    lo = (x - hi.astype(jnp.float32)).astype(jnp.bfloat16)
    return hi, lo


def dot(a, b):
    return jnp.dot(a, b, preferred_element_type=jnp.float32)


def three_parts(pieces):
    split = [split_bf16(piece) for piece in pieces]
    hi = [s[0] for s in split]
    lo = [s[1] for s in split]
    return jnp.concatenate(hi + hi + lo, axis=0)


def find_block(owner_ref, my_slot):
    return lax.fori_loop(
        0, owner_ref.shape[0], lambda i, found: jnp.where(owner_ref[i] == my_slot, i, found), 0
    )


def faces_kernel(owner_ref, rows_ref, part_ref, q_ref, held_ref, out_ref, sems):
    nvar, rows, x_length = held_ref.shape[1:]
    copies = [pltpu.make_async_copy(q_ref.at[0, v], held_ref.at[0, v], sems.at[v]) for v in range(nvar)]
    for copy in copies:
        copy.start()
    live_rows = rows_ref[find_block(owner_ref, lax.axis_index("blk"))]
    y_index = lax.axis_index("line") * rows + lax.broadcasted_iota(jnp.int32, (GHOST, rows), 1)
    live = y_index < live_rows
    for m in range(2):
        out_ref[0, m, GHOST * nvar :, :] = jnp.zeros((FACE_ROWS - GHOST * nvar, rows), jnp.float32)
    for v in range(nvar):
        copies[v].wait()
        low = jnp.transpose(held_ref[0, v, :, :LANES])[:GHOST]
        high = jnp.transpose(held_ref[0, v, :, x_length - LANES :])[LANES - GHOST :]
        out_ref[0, 0, GHOST * v : GHOST * (v + 1), :] = jnp.where(live, low, 0.0)
        out_ref[0, 1, GHOST * v : GHOST * (v + 1), :] = jnp.where(live, high, 0.0)


def part_kernel(low, q_ref, out_ref, sem):
    copy = pltpu.make_async_copy(q_ref.at[:, low : low + out_ref.shape[1]], out_ref, sem)
    copy.start()
    copy.wait()


def weights_kernel(
    lines,
    owner_ref,
    rows_ref,
    coef_ref,
    yop_ref,
    wown_ref,
    wnear_ref,
    wdirect_ref,
    wsibling_ref,
    wsend_ref,
    nu_ref,
    columns_ref,
    turned_ref,
    theirs_ref,
    pieces_hi_ref,
    pieces_lo_ref,
    sems,
):
    y_length = yop_ref.shape[0]
    rows = y_length // lines
    line_pos = lax.axis_index("line")
    other = jnp.bitwise_xor(line_pos, 1)
    shifts = range(2, lines, 2)
    targets = [lax.rem(line_pos + s, lines) for s in shifts]

    def column(d, line):
        return pl.ds(pl.multiple_of(d * y_length + (line * rows) // LANES * LANES, LANES), LANES)

    copies = []
    for d in range(2):
        source = yop_ref.at[:, column(d, line_pos)]
        copies.append(pltpu.make_async_copy(source, columns_ref.at[d], sems.at[d]))
    direct = [lax.rem(line_pos + lines - s, lines) for s in shifts]
    others = [(target, [line_pos, other]) for target in targets] + [(other, [line_pos] + direct)]
    for j, (target, sources) in enumerate(others):
        for d in range(2):
            for i, line in enumerate(sources):
                source = yop_ref.at[pl.ds(pl.multiple_of(line * rows, 8), rows), column(d, target)]
                goal = theirs_ref.at[j, d, i * rows : (i + 1) * rows]
                copies.append(pltpu.make_async_copy(source, goal, sems.at[len(copies)]))
    for copy in copies:
        copy.start()

    live_rows = rows_ref[find_block(owner_ref, lax.axis_index("blk"))]
    for v in range(nu_ref.shape[0]):
        nu_ref[v] = jnp.full(nu_ref.shape[1:], coef_ref[v], jnp.float32)
    for copy in copies:
        copy.wait()

    shape = (rows, y_length)
    live_in = lax.broadcasted_iota(jnp.int32, shape, 1) < live_rows
    live_out = line_pos * rows + lax.broadcasted_iota(jnp.int32, shape, 0) < live_rows
    offset = pl.multiple_of(lax.rem(line_pos * rows, LANES), 8)
    for d in range(2):
        turned_ref[d] = jnp.transpose(columns_ref[d])
        mine = turned_ref[d, pl.ds(offset, rows), :]
        hi, lo = split_bf16(jnp.where(live_in & live_out, SECTION_STEP * mine, 0.0))
        for p in range(lines):
            pieces_hi_ref[p, d * rows : (d + 1) * rows] = hi[:, p * rows : (p + 1) * rows]
            pieces_lo_ref[p, d * rows : (d + 1) * rows] = lo[:, p * rows : (p + 1) * rows]

    def gather(ref, places):
        hi = [pieces_hi_ref[p] for p in places]
        lo = [pieces_lo_ref[p] for p in places]
        ref[...] = jnp.concatenate(hi + lo + hi, axis=1)

    gather(wown_ref, [line_pos])
    gather(wnear_ref, [other])
    gather(wdirect_ref, direct)

    for j, (target, sources) in enumerate(others):
        depth = len(sources) * rows
        shape = (rows, rows)
        ins = [line * rows + lax.broadcasted_iota(jnp.int32, shape, 1) for line in sources]
        live_in = jnp.concatenate(ins, axis=1) < live_rows
        live_out = target * rows + lax.broadcasted_iota(jnp.int32, live_in.shape, 0) < live_rows
        offset = pl.multiple_of(lax.rem(target * rows, LANES), 8)
        goal = wsend_ref.at[j] if j < len(targets) else wsibling_ref
        for d in range(2):
            turned_ref[d, :, :depth] = jnp.transpose(theirs_ref[j, d, :depth])
            mine = turned_ref[d, pl.ds(offset, rows), :depth]
            hi, lo = split_bf16(jnp.where(live_in & live_out, SECTION_STEP * mine, 0.0))
            goal[d * rows : (d + 1) * rows] = jnp.concatenate([hi, lo, hi], axis=1)


def own_kernel(
    owner_ref,
    rows_ref,
    coef_ref,
    wown_ref,
    q_ref,
    tile_ref,
    dx_ref,
    dxx_ref,
    out_ref,
    hi_ref,
    lo_ref,
):
    nvar, rows, _ = q_ref.shape[1:]
    live_rows = rows_ref[find_block(owner_ref, lax.axis_index("blk"))]

    @pl.when(pl.program_id(0) == 0)
    def _():
        for v in range(nvar):
            hi, lo = split_bf16(q_ref[0, v])
            hi_ref[v * rows : (v + 1) * rows] = hi
            lo_ref[v * rows : (v + 1) * rows] = lo

    def derivative(op_ref):
        hi, lo = split_bf16(op_ref[...])
        return dot(hi_ref[...], hi) + dot(lo_ref[...], hi) + dot(hi_ref[...], lo)

    dx = derivative(dx_ref)
    dxx = derivative(dxx_ref)
    u, w = tile_ref[0, 0], tile_ref[0, 1]
    live = lax.axis_index("line") * rows + lax.broadcasted_iota(jnp.int32, u.shape, 0) < live_rows
    for v in range(nvar):
        here = slice(v * rows, (v + 1) * rows)
        dy = dot(wown_ref[...], three_parts([tile_ref[0, v]]))
        rhs = coef_ref[v] * dxx[here] - u * dx[here]
        if v == 1:
            rhs = rhs + coef_ref[nvar] * tile_ref[0, 3] + coef_ref[nvar + 1] * tile_ref[0, 4]
        value = jnp.where(live, tile_ref[0, v] + SECTION_STEP * rhs, 0.0)
        out_ref[0, v] = value + coef_ref[v] * dy[rows:] - w * dy[:rows]


def near_kernel(
    face_count,
    owner_ref,
    link_ref,
    side_ref,
    rows_ref,
    gop_ref,
    wnear_ref,
    wdirect_ref,
    nu_ref,
    q_ref,
    base_ref,
    *refs,
):
    near, refs = refs[: len(SENT)], refs[len(SENT) :]
    faces, refs = refs[:face_count], refs[face_count:]
    *refs, out_ref, left_ref, done_ref, sems = refs
    count = (len(refs) - len(RAW)) // 2
    raw = {}
    for low, high in (FIRST, SECOND):
        direct, refs = refs[:count], refs[count:]
        for v in range(low, high):
            raw[v] = [ref.at[0, v - low] for ref in direct] + [refs[v - low].at[0, 0]]
        refs = refs[high - low :]
    nvar, rows, x_length = q_ref.shape[1:]
    my_slot = lax.axis_index("blk")
    my_block = find_block(owner_ref, my_slot)
    sides = [side_ref[m, my_block] for m in range(2)]
    live_rows = rows_ref[my_block]
    y_index = lax.axis_index("line") * rows + lax.broadcasted_iota(jnp.int32, (FACE_ROWS, rows), 1)
    scale = jnp.where(y_index < live_rows, SECTION_STEP, 0.0)

    planes = []
    for m in range(2):
        place = jnp.bitwise_xor(owner_ref[link_ref[m, my_block]], my_slot)
        plane, first = faces[0][0, sides[m]], 1
        for ref in faces[1:]:
            count = ref.shape[0]
            at = jnp.clip(place - first, 0, count - 1)
            plane = jnp.where(place >= first, ref[at, sides[m]], plane)
            first += count
        planes.append(plane * scale)

    def ghost_rows(g):
        parts = []
        for m in range(2):
            straight = g[GHOST * m : GHOST * (m + 1)]
            turned = jnp.concatenate([straight[2:3], straight[1:2], straight[0:1]], axis=0)
            parts.append(jnp.where(sides[m] == m, turned, straight))
        hi, lo = split_bf16(jnp.concatenate(parts, axis=0))
        pad = jnp.zeros((LANES - 6 * GHOST, hi.shape[1]), jnp.float32)
        stacked = [hi.astype(jnp.float32), hi.astype(jnp.float32), lo.astype(jnp.float32)]
        return jnp.concatenate(stacked + [pad], axis=0).astype(jnp.bfloat16)

    operator = ghost_rows(gop_ref[...])
    pad = jnp.zeros((LANES - 6 * GHOST, rows), jnp.float32)
    copies = []
    for v in RAW + SENT:
        parts = []
        for m in range(2):
            part = planes[m][GHOST * v : GHOST * (v + 1)]
            if v == 0:
                part = jnp.where(sides[m] == m, -part, part)
            parts.append(part)
        hi, lo = split_bf16(jnp.concatenate(parts, axis=0))
        stacked = [hi.astype(jnp.float32), lo.astype(jnp.float32), hi.astype(jnp.float32)]
        ghost = jnp.transpose(jnp.concatenate(stacked + [pad], axis=0)).astype(jnp.bfloat16)
        dx = dot(ghost, operator)
        if v in SENT:
            dy = dot(wnear_ref[...], three_parts([near[SENT.index(v)][0, 0]]))
        else:
            *direct, from_sibling = raw[v]
            dy = dot(wdirect_ref[...], three_parts([ref[...] for ref in direct]))
        second = nu_ref[v, 0:1] * (dx[:, x_length:] + dy[rows:])
        value = base_ref[0, v] + second - q_ref[0, 0] * dx[:, :x_length] - q_ref[0, 1] * dy[:rows]
        if v in SENT:
            left_ref[0, SENT.index(v)] = value
            continue
        i = RAW.index(v)
        done_ref[i] = value + from_sibling[...]
        copies.append(pltpu.make_async_copy(done_ref.at[i], out_ref.at[0, v], sems.at[i]))
        copies[-1].start()
    for copy in copies:
        copy.wait()


def send_kernel(wsend_ref, nu_ref, q_ref, *refs):
    count = wsend_ref.shape[0]
    far_v, near, out = refs[:count], refs[count : count + len(SENT)], refs[count + len(SENT) :]
    rows = q_ref.shape[2]
    for j in range(count):
        for i, v in enumerate(SENT):
            dy = dot(wsend_ref[j], three_parts([q_ref[0, v], near[i][0, 0]]))
            out[j][0, i] = nu_ref[v, 0:1] * dy[rows:] - far_v[j][0, 0] * dy[:rows]


def sibling_kernel(low, high, w_ref, nu_ref, q_ref, near_v_ref, *refs):
    direct, out = refs[: low - high], refs[low - high :]
    rows = q_ref.shape[2]
    for i in range(high - low):
        v = low + i
        dy = dot(w_ref[...], three_parts([q_ref[0, v]] + [piece[0, i] for piece in direct]))
        out[i][0, 0] = nu_ref[v, 0:1] * dy[rows:] - near_v_ref[0, 0] * dy[:rows]


def last_kernel(left_ref, *refs):
    results, (_, out_ref, done_ref, sems) = refs[:-4], refs[-4:]
    copies = []
    for i, v in enumerate(SENT):
        done_ref[i] = left_ref[0, i] + sum(piece[0, i] for piece in results)
        copies.append(pltpu.make_async_copy(done_ref.at[i], out_ref.at[0, v], sems.at[i]))
        copies[-1].start()
    for copy in copies:
        copy.wait()


def smem():
    return pl.BlockSpec(memory_space=SMEM)


def kept():
    return pl.BlockSpec(memory_space=VMEM)


def held(array):
    return pltpu.with_memory_space_constraint(array, VMEM)


def on_device(
    slots,
    lines,
    flow_state,
    block_owner,
    link_block,
    link_side,
    rows_live,
    x_operator,
    ghost_operator,
    y_operator,
    coefficients,
):
    _, nvar, rows, x_length = flow_state.shape
    y_length = lines * rows
    limit = pltpu.CompilerParams(vmem_limit_bytes=16 * 1024 * 1024)
    small = pl.CostEstimate(flops=1, bytes_accessed=1, transcendentals=0)
    state_shape = jax.ShapeDtypeStruct(flow_state.shape, jnp.float32)
    sibling = [(i, i ^ 1) for i in range(lines)]
    shifts = range(2, lines, 2)

    def across(array):
        return [lax.ppermute(array, "line", [(i, (i + s) % lines) for i in range(lines)]) for s in shifts]

    low, high = FIRST
    part = pl.pallas_call(
        functools.partial(part_kernel, low),
        in_specs=[pl.BlockSpec(memory_space=pl.ANY)],
        out_specs=pl.BlockSpec(memory_space=VMEM),
        out_shape=jax.ShapeDtypeStruct((1, high - low, rows, x_length), jnp.float32),
        scratch_shapes=[pltpu.SemaphoreType.DMA],
        compiler_params=limit,
        cost_estimate=small,
        name="part",
    )(pltpu.with_memory_space_constraint(flow_state, HBM))
    direct_first = across(part)

    in_hbm = pltpu.with_memory_space_constraint(flow_state, HBM)
    flow_state, faces = pl.pallas_call(
        faces_kernel,
        in_specs=[smem(), smem(), kept(), pl.BlockSpec(memory_space=pl.ANY)],
        out_specs=[kept(), kept()],
        out_shape=[state_shape, jax.ShapeDtypeStruct((1, 2, FACE_ROWS, rows), jnp.float32)],
        scratch_shapes=[pltpu.SemaphoreType.DMA((nvar,))],
        compiler_params=limit,
        cost_estimate=small,
        name="faces",
    )(block_owner, rows_live, held(part), in_hbm)
    second = flow_state[:, SECOND[0] : SECOND[1]]
    direct_second = across(second)
    near = [lax.ppermute(flow_state[:, v : v + 1], "line", sibling) for v in SENT]

    w_near = jax.ShapeDtypeStruct((2 * rows, 3 * rows), jnp.bfloat16)
    w_far = jax.ShapeDtypeStruct((2 * rows, 3 * len(shifts) * rows), jnp.bfloat16)
    w_sibling = jax.ShapeDtypeStruct((2 * rows, 3 * (1 + len(shifts)) * rows), jnp.bfloat16)
    w_send = jax.ShapeDtypeStruct((len(shifts), 2 * rows, 6 * rows), jnp.bfloat16)
    nu = jax.ShapeDtypeStruct((nvar, 8, x_length), jnp.float32)
    w_own, w_near, w_direct, w_sibling, w_send, nu = pl.pallas_call(
        functools.partial(weights_kernel, lines),
        in_specs=[smem()] * 3 + [pl.BlockSpec(memory_space=pl.ANY)],
        out_specs=[kept()] * 6,
        out_shape=[w_near, w_near, w_far, w_sibling, w_send, nu],
        scratch_shapes=[
            pltpu.VMEM((2, y_length, LANES), jnp.float32),
            pltpu.VMEM((2, LANES, y_length), jnp.float32),
            pltpu.VMEM((len(shifts) + 1, 2, max(2, lines // 2) * rows, LANES), jnp.float32),
            pltpu.VMEM((lines, 2 * rows, rows), jnp.bfloat16),
            pltpu.VMEM((lines, 2 * rows, rows), jnp.bfloat16),
            pltpu.SemaphoreType.DMA((2 + 4 * len(shifts) + lines,)),
        ],
        compiler_params=limit,
        cost_estimate=small,
        name="weights",
    )(block_owner, rows_live, coefficients, pltpu.with_memory_space_constraint(y_operator, HBM))

    tiles = x_length // TILE
    def own_terms(w_own):
        return pl.pallas_call(
            own_kernel,
            grid=(tiles,),
            in_specs=[smem()] * 3
            + [
                pl.BlockSpec(w_own.shape, lambda n: (0, 0)),
                pl.BlockSpec((1, nvar, rows, x_length), lambda n: (0, 0, 0, 0)),
                pl.BlockSpec((1, nvar, rows, TILE), lambda n: (0, 0, 0, n)),
                pl.BlockSpec((x_length, TILE), lambda n: (0, n)),
                pl.BlockSpec((x_length, TILE), lambda n: (0, n + tiles)),
            ],
            out_specs=pl.BlockSpec((1, nvar, rows, TILE), lambda n: (0, 0, 0, n)),
            out_shape=state_shape,
            scratch_shapes=[
                pltpu.VMEM((nvar * rows, x_length), jnp.bfloat16),
                pltpu.VMEM((nvar * rows, x_length), jnp.bfloat16),
            ],
            compiler_params=limit,
            cost_estimate=small,
            name="own_terms",
        )(
            block_owner,
            rows_live,
            coefficients,
            w_own,
            flow_state,
            flow_state,
            *[pltpu.with_memory_space_constraint(x_operator, HBM)] * 2,
        )

    far_v = [direct_first[shifts.index(lines - s)] for s in shifts]
    sent = jax.ShapeDtypeStruct((1, len(SENT), rows, x_length), jnp.float32)
    send = pl.pallas_call(
        send_kernel,
        in_specs=[kept()] * (3 + len(SENT) + len(shifts)),
        out_specs=[kept()] * len(shifts),
        out_shape=[sent] * len(shifts),
        compiler_params=limit,
        cost_estimate=small,
        name="send_terms",
    )
    arrived = [faces]
    held_faces, step = faces, 1
    while step < slots:
        there = lax.ppermute(held_faces, "blk", [(i, i ^ step) for i in range(slots)])
        if step == 1:
            there, w_own, own = lax.optimization_barrier((there, w_own, flow_state))
            near_v = lax.ppermute(own[:, 1:2], "line", sibling)
        elif step == 2:
            w_send, *_ = lax.optimization_barrier((w_send, there))
            results = send(*map(held, (w_send, nu, flow_state, *far_v, *near)))
            direct_first, *_ = lax.optimization_barrier((direct_first, *results))
            direct_second, *_ = lax.optimization_barrier((direct_second, *results))
            w_own, *_ = lax.optimization_barrier((w_own, *results))
            state = own_terms(w_own)
        arrived.append(there)
        step *= 2
        if step < slots:
            held_faces = jnp.concatenate([held_faces, there], axis=0)

    results = [
        lax.ppermute(result, "line", [(i, (i + s) % lines) for i in range(lines)])
        for s, result in zip(shifts, results)
    ]

    def sibling_terms(part, direct):
        operands = [*map(held, (w_sibling, nu, flow_state, near_v, *direct))]
        low, high = part
        results = pl.pallas_call(
            functools.partial(sibling_kernel, low, high),
            in_specs=[kept()] * len(operands),
            out_specs=[kept()] * (high - low),
            out_shape=[jax.ShapeDtypeStruct((1, 1, rows, x_length), jnp.float32)] * (high - low),
            compiler_params=limit,
            cost_estimate=small,
            name="sibling_terms",
        )(*operands)
        return [*direct, *(lax.ppermute(result, "line", sibling) for result in results)]

    direct_second, *_ = lax.optimization_barrier((direct_second, state, *arrived))
    pieces = sibling_terms(FIRST, direct_first) + sibling_terms(SECOND, direct_second)

    anywhere = pl.BlockSpec(memory_space=pl.ANY)
    result, left = pl.pallas_call(
        functools.partial(near_kernel, len(arrived)),
        in_specs=[smem()] * 4 + [kept()] * (6 + len(SENT) + len(arrived) + len(pieces)),
        out_specs=[anywhere, kept()],
        out_shape=[state_shape, sent],
        scratch_shapes=[
            pltpu.VMEM((len(RAW), rows, x_length), jnp.float32),
            pltpu.SemaphoreType.DMA((len(RAW),)),
        ],
        compiler_params=limit,
        cost_estimate=small,
        name="near_terms",
    )(
        block_owner,
        link_block.T,
        link_side.T,
        rows_live,
        *map(held, (ghost_operator, w_near, w_direct, nu, flow_state, state, *near, *arrived, *pieces)),
    )

    operands = [*map(held, (left, *results))]
    return pl.pallas_call(
        last_kernel,
        in_specs=[kept()] * len(operands) + [anywhere],
        out_specs=anywhere,
        out_shape=state_shape,
        input_output_aliases={len(operands): 0},
        scratch_shapes=[pltpu.VMEM(sent.shape[1:], jnp.float32), pltpu.SemaphoreType.DMA((len(SENT),))],
        compiler_params=limit,
        cost_estimate=small,
        name="last_terms",
    )(*operands, result)


def solution(mesh):
    return jax.shard_map(
        functools.partial(on_device, mesh.shape["blk"], mesh.shape["line"]),
        mesh=mesh,
        in_specs=(P("blk", None, "line", None), P(), P(), P(), P(), P(), P(), P(), P()),
        out_specs=P("blk", None, "line", None),
        check_vma=False,
    )
```

```python
import functools

import jax
import jax.numpy as jnp
from jax import lax
from jax.experimental import pallas as pl
from jax.experimental.pallas import tpu as pltpu
from jax.sharding import PartitionSpec as P

GHOST = 3
SECTION_STEP = 0.3
FACE_ROWS = 16
TILE = 256
LANES = 128
FIRST, SECOND = (1, 2), (2, 4)
RAW = tuple(range(FIRST[0], SECOND[1]))
SENT = (0, 4)

SMEM = pltpu.MemorySpace.SMEM
VMEM = pltpu.MemorySpace.VMEM
HBM = pltpu.MemorySpace.HBM


def split_bf16(x):
    hi = x.astype(jnp.bfloat16)
    lo = (x - hi.astype(jnp.float32)).astype(jnp.bfloat16)
    return hi, lo


def dot(a, b):
    return jnp.dot(a, b, preferred_element_type=jnp.float32)


def three_parts(pieces):
    split = [split_bf16(piece) for piece in pieces]
    hi = [s[0] for s in split]
    lo = [s[1] for s in split]
    return jnp.concatenate(hi + hi + lo, axis=0)


def find_block(owner_ref, my_slot):
    return lax.fori_loop(
        0, owner_ref.shape[0], lambda i, found: jnp.where(owner_ref[i] == my_slot, i, found), 0
    )


def faces_kernel(owner_ref, rows_ref, part_ref, q_ref, held_ref, out_ref, sems):
    nvar, rows, x_length = held_ref.shape[1:]
    copies = [pltpu.make_async_copy(q_ref.at[0, v], held_ref.at[0, v], sems.at[v]) for v in range(nvar)]
    for copy in copies:
        copy.start()
    live_rows = rows_ref[find_block(owner_ref, lax.axis_index("blk"))]
    y_index = lax.axis_index("line") * rows + lax.broadcasted_iota(jnp.int32, (GHOST, rows), 1)
    live = y_index < live_rows
    for m in range(2):
        out_ref[0, m, GHOST * nvar :, :] = jnp.zeros((FACE_ROWS - GHOST * nvar, rows), jnp.float32)
    for v in range(nvar):
        copies[v].wait()
        low = jnp.transpose(held_ref[0, v, :, :LANES])[:GHOST]
        high = jnp.transpose(held_ref[0, v, :, x_length - LANES :])[LANES - GHOST :]
        out_ref[0, 0, GHOST * v : GHOST * (v + 1), :] = jnp.where(live, low, 0.0)
        out_ref[0, 1, GHOST * v : GHOST * (v + 1), :] = jnp.where(live, high, 0.0)


def part_kernel(low, q_ref, out_ref, sem):
    copy = pltpu.make_async_copy(q_ref.at[:, low : low + out_ref.shape[1]], out_ref, sem)
    copy.start()
    copy.wait()


def weights_kernel(
    lines,
    owner_ref,
    rows_ref,
    coef_ref,
    yop_ref,
    wown_ref,
    wnear_ref,
    wdirect_ref,
    wsibling_ref,
    wsend_ref,
    nu_ref,
    columns_ref,
    turned_ref,
    theirs_ref,
    pieces_hi_ref,
    pieces_lo_ref,
    sems,
):
    y_length = yop_ref.shape[0]
    rows = y_length // lines
    line_pos = lax.axis_index("line")
    other = jnp.bitwise_xor(line_pos, 1)
    shifts = range(2, lines, 2)
    targets = [lax.rem(line_pos + s, lines) for s in shifts]

    def column(d, line):
        return pl.ds(pl.multiple_of(d * y_length + (line * rows) // LANES * LANES, LANES), LANES)

    copies = []
    for d in range(2):
        source = yop_ref.at[:, column(d, line_pos)]
        copies.append(pltpu.make_async_copy(source, columns_ref.at[d], sems.at[d]))
    direct = [lax.rem(line_pos + lines - s, lines) for s in shifts]
    others = [(target, [line_pos, other]) for target in targets] + [(other, [line_pos] + direct)]
    for j, (target, sources) in enumerate(others):
        for d in range(2):
            for i, line in enumerate(sources):
                source = yop_ref.at[pl.ds(pl.multiple_of(line * rows, 8), rows), column(d, target)]
                goal = theirs_ref.at[j, d, i * rows : (i + 1) * rows]
                copies.append(pltpu.make_async_copy(source, goal, sems.at[len(copies)]))
    for copy in copies:
        copy.start()

    live_rows = rows_ref[find_block(owner_ref, lax.axis_index("blk"))]
    for v in range(nu_ref.shape[0]):
        nu_ref[v] = jnp.full(nu_ref.shape[1:], coef_ref[v], jnp.float32)
    for copy in copies:
        copy.wait()

    shape = (rows, y_length)
    live_in = lax.broadcasted_iota(jnp.int32, shape, 1) < live_rows
    live_out = line_pos * rows + lax.broadcasted_iota(jnp.int32, shape, 0) < live_rows
    offset = pl.multiple_of(lax.rem(line_pos * rows, LANES), 8)
    for d in range(2):
        turned_ref[d] = jnp.transpose(columns_ref[d])
        mine = turned_ref[d, pl.ds(offset, rows), :]
        hi, lo = split_bf16(jnp.where(live_in & live_out, SECTION_STEP * mine, 0.0))
        for p in range(lines):
            pieces_hi_ref[p, d * rows : (d + 1) * rows] = hi[:, p * rows : (p + 1) * rows]
            pieces_lo_ref[p, d * rows : (d + 1) * rows] = lo[:, p * rows : (p + 1) * rows]

    def gather(ref, places):
        hi = [pieces_hi_ref[p] for p in places]
        lo = [pieces_lo_ref[p] for p in places]
        ref[...] = jnp.concatenate(hi + lo + hi, axis=1)

    gather(wown_ref, [line_pos])
    gather(wnear_ref, [other])
    gather(wdirect_ref, direct)

    for j, (target, sources) in enumerate(others):
        depth = len(sources) * rows
        shape = (rows, rows)
        ins = [line * rows + lax.broadcasted_iota(jnp.int32, shape, 1) for line in sources]
        live_in = jnp.concatenate(ins, axis=1) < live_rows
        live_out = target * rows + lax.broadcasted_iota(jnp.int32, live_in.shape, 0) < live_rows
        offset = pl.multiple_of(lax.rem(target * rows, LANES), 8)
        goal = wsend_ref.at[j] if j < len(targets) else wsibling_ref
        for d in range(2):
            turned_ref[d, :, :depth] = jnp.transpose(theirs_ref[j, d, :depth])
            mine = turned_ref[d, pl.ds(offset, rows), :depth]
            hi, lo = split_bf16(jnp.where(live_in & live_out, SECTION_STEP * mine, 0.0))
            goal[d * rows : (d + 1) * rows] = jnp.concatenate([hi, lo, hi], axis=1)


def own_kernel(
    owner_ref,
    rows_ref,
    coef_ref,
    wown_ref,
    q_ref,
    tile_ref,
    dx_ref,
    dxx_ref,
    out_ref,
    hi_ref,
    lo_ref,
):
    nvar, rows, _ = q_ref.shape[1:]
    live_rows = rows_ref[find_block(owner_ref, lax.axis_index("blk"))]

    @pl.when(pl.program_id(0) == 0)
    def _():
        for v in range(nvar):
            hi, lo = split_bf16(q_ref[0, v])
            hi_ref[v * rows : (v + 1) * rows] = hi
            lo_ref[v * rows : (v + 1) * rows] = lo

    def derivative(op_ref):
        hi, lo = split_bf16(op_ref[...])
        return dot(hi_ref[...], hi) + dot(lo_ref[...], hi) + dot(hi_ref[...], lo)

    dx = derivative(dx_ref)
    dxx = derivative(dxx_ref)
    u, w = tile_ref[0, 0], tile_ref[0, 1]
    live = lax.axis_index("line") * rows + lax.broadcasted_iota(jnp.int32, u.shape, 0) < live_rows
    for v in range(nvar):
        here = slice(v * rows, (v + 1) * rows)
        dy = dot(wown_ref[...], three_parts([tile_ref[0, v]]))
        rhs = coef_ref[v] * dxx[here] - u * dx[here]
        if v == 1:
            rhs = rhs + coef_ref[nvar] * tile_ref[0, 3] + coef_ref[nvar + 1] * tile_ref[0, 4]
        value = jnp.where(live, tile_ref[0, v] + SECTION_STEP * rhs, 0.0)
        out_ref[0, v] = value + coef_ref[v] * dy[rows:] - w * dy[:rows]


def near_kernel(
    face_count,
    owner_ref,
    link_ref,
    side_ref,
    rows_ref,
    gop_ref,
    wnear_ref,
    wdirect_ref,
    nu_ref,
    q_ref,
    base_ref,
    *refs,
):
    near, refs = refs[: len(SENT)], refs[len(SENT) :]
    faces, refs = refs[:face_count], refs[face_count:]
    *refs, out_ref, left_ref, done_ref, sems = refs
    count = (len(refs) - len(RAW)) // 2
    raw = {}
    for low, high in (FIRST, SECOND):
        direct, refs = refs[:count], refs[count:]
        for v in range(low, high):
            raw[v] = [ref.at[0, v - low] for ref in direct] + [refs[v - low].at[0, 0]]
        refs = refs[high - low :]
    nvar, rows, x_length = q_ref.shape[1:]
    my_slot = lax.axis_index("blk")
    my_block = find_block(owner_ref, my_slot)
    sides = [side_ref[m, my_block] for m in range(2)]
    live_rows = rows_ref[my_block]
    y_index = lax.axis_index("line") * rows + lax.broadcasted_iota(jnp.int32, (FACE_ROWS, rows), 1)
    scale = jnp.where(y_index < live_rows, SECTION_STEP, 0.0)

    planes = []
    for m in range(2):
        place = jnp.bitwise_xor(owner_ref[link_ref[m, my_block]], my_slot)
        plane, first = faces[0][0, sides[m]], 1
        for ref in faces[1:]:
            count = ref.shape[0]
            at = jnp.clip(place - first, 0, count - 1)
            plane = jnp.where(place >= first, ref[at, sides[m]], plane)
            first += count
        planes.append(plane * scale)

    def ghost_rows(g):
        parts = []
        for m in range(2):
            straight = g[GHOST * m : GHOST * (m + 1)]
            turned = jnp.concatenate([straight[2:3], straight[1:2], straight[0:1]], axis=0)
            parts.append(jnp.where(sides[m] == m, turned, straight))
        hi, lo = split_bf16(jnp.concatenate(parts, axis=0))
        pad = jnp.zeros((LANES - 6 * GHOST, hi.shape[1]), jnp.float32)
        stacked = [hi.astype(jnp.float32), hi.astype(jnp.float32), lo.astype(jnp.float32)]
        return jnp.concatenate(stacked + [pad], axis=0).astype(jnp.bfloat16)

    operator = ghost_rows(gop_ref[...])
    pad = jnp.zeros((LANES - 6 * GHOST, rows), jnp.float32)
    copies = []
    for v in RAW + SENT:
        parts = []
        for m in range(2):
            part = planes[m][GHOST * v : GHOST * (v + 1)]
            if v == 0:
                part = jnp.where(sides[m] == m, -part, part)
            parts.append(part)
        hi, lo = split_bf16(jnp.concatenate(parts, axis=0))
        stacked = [hi.astype(jnp.float32), lo.astype(jnp.float32), hi.astype(jnp.float32)]
        ghost = jnp.transpose(jnp.concatenate(stacked + [pad], axis=0)).astype(jnp.bfloat16)
        dx = dot(ghost, operator)
        if v in SENT:
            dy = dot(wnear_ref[...], three_parts([near[SENT.index(v)][0, 0]]))
        else:
            *direct, from_sibling = raw[v]
            dy = dot(wdirect_ref[...], three_parts([ref[...] for ref in direct]))
        second = nu_ref[v, 0:1] * (dx[:, x_length:] + dy[rows:])
        value = base_ref[0, v] + second - q_ref[0, 0] * dx[:, :x_length] - q_ref[0, 1] * dy[:rows]
        if v in SENT:
            left_ref[0, SENT.index(v)] = value
            continue
        i = RAW.index(v)
        done_ref[i] = value + from_sibling[...]
        copies.append(pltpu.make_async_copy(done_ref.at[i], out_ref.at[0, v], sems.at[i]))
        copies[-1].start()
    for copy in copies:
        copy.wait()


def send_kernel(wsend_ref, nu_ref, q_ref, *refs):
    count = wsend_ref.shape[0]
    far_v, near, out = refs[:count], refs[count : count + len(SENT)], refs[count + len(SENT) :]
    rows = q_ref.shape[2]
    for j in range(count):
        for i, v in enumerate(SENT):
            dy = dot(wsend_ref[j], three_parts([q_ref[0, v], near[i][0, 0]]))
            out[j][0, i] = nu_ref[v, 0:1] * dy[rows:] - far_v[j][0, 0] * dy[:rows]


def sibling_kernel(low, high, w_ref, nu_ref, q_ref, near_v_ref, *refs):
    direct, out = refs[: low - high], refs[low - high :]
    rows = q_ref.shape[2]
    for i in range(high - low):
        v = low + i
        dy = dot(w_ref[...], three_parts([q_ref[0, v]] + [piece[0, i] for piece in direct]))
        out[i][0, 0] = nu_ref[v, 0:1] * dy[rows:] - near_v_ref[0, 0] * dy[:rows]


def last_kernel(left_ref, *refs):
    results, (_, out_ref, done_ref, sems) = refs[:-4], refs[-4:]
    copies = []
    for i, v in enumerate(SENT):
        done_ref[i] = left_ref[0, i] + sum(piece[0, i] for piece in results)
        copies.append(pltpu.make_async_copy(done_ref.at[i], out_ref.at[0, v], sems.at[i]))
        copies[-1].start()
    for copy in copies:
        copy.wait()


def smem():
    return pl.BlockSpec(memory_space=SMEM)


def kept():
    return pl.BlockSpec(memory_space=VMEM)


def held(array):
    return pltpu.with_memory_space_constraint(array, VMEM)


def on_device(
    slots,
    lines,
    flow_state,
    block_owner,
    link_block,
    link_side,
    rows_live,
    x_operator,
    ghost_operator,
    y_operator,
    coefficients,
):
    _, nvar, rows, x_length = flow_state.shape
    y_length = lines * rows
    limit = pltpu.CompilerParams(vmem_limit_bytes=16 * 1024 * 1024)
    small = pl.CostEstimate(flops=1, bytes_accessed=1, transcendentals=0)
    state_shape = jax.ShapeDtypeStruct(flow_state.shape, jnp.float32)
    sibling = [(i, i ^ 1) for i in range(lines)]
    shifts = range(2, lines, 2)

    def across(array):
        return [lax.ppermute(array, "line", [(i, (i + s) % lines) for i in range(lines)]) for s in shifts]

    low, high = FIRST
    part = pl.pallas_call(
        functools.partial(part_kernel, low),
        in_specs=[pl.BlockSpec(memory_space=pl.ANY)],
        out_specs=pl.BlockSpec(memory_space=VMEM),
        out_shape=jax.ShapeDtypeStruct((1, high - low, rows, x_length), jnp.float32),
        scratch_shapes=[pltpu.SemaphoreType.DMA],
        compiler_params=limit,
        cost_estimate=small,
        name="part",
    )(pltpu.with_memory_space_constraint(flow_state, HBM))
    direct_first = across(part)

    in_hbm = pltpu.with_memory_space_constraint(flow_state, HBM)
    flow_state, faces = pl.pallas_call(
        faces_kernel,
        in_specs=[smem(), smem(), kept(), pl.BlockSpec(memory_space=pl.ANY)],
        out_specs=[kept(), kept()],
        out_shape=[state_shape, jax.ShapeDtypeStruct((1, 2, FACE_ROWS, rows), jnp.float32)],
        scratch_shapes=[pltpu.SemaphoreType.DMA((nvar,))],
        compiler_params=limit,
        cost_estimate=small,
        name="faces",
    )(block_owner, rows_live, held(part), in_hbm)
    second = flow_state[:, SECOND[0] : SECOND[1]]
    direct_second = across(second)
    near = [lax.ppermute(flow_state[:, v : v + 1], "line", sibling) for v in SENT]

    w_near = jax.ShapeDtypeStruct((2 * rows, 3 * rows), jnp.bfloat16)
    w_far = jax.ShapeDtypeStruct((2 * rows, 3 * len(shifts) * rows), jnp.bfloat16)
    w_sibling = jax.ShapeDtypeStruct((2 * rows, 3 * (1 + len(shifts)) * rows), jnp.bfloat16)
    w_send = jax.ShapeDtypeStruct((len(shifts), 2 * rows, 6 * rows), jnp.bfloat16)
    nu = jax.ShapeDtypeStruct((nvar, 8, x_length), jnp.float32)
    w_own, w_near, w_direct, w_sibling, w_send, nu = pl.pallas_call(
        functools.partial(weights_kernel, lines),
        in_specs=[smem()] * 3 + [pl.BlockSpec(memory_space=pl.ANY)],
        out_specs=[kept()] * 6,
        out_shape=[w_near, w_near, w_far, w_sibling, w_send, nu],
        scratch_shapes=[
            pltpu.VMEM((2, y_length, LANES), jnp.float32),
            pltpu.VMEM((2, LANES, y_length), jnp.float32),
            pltpu.VMEM((len(shifts) + 1, 2, max(2, lines // 2) * rows, LANES), jnp.float32),
            pltpu.VMEM((lines, 2 * rows, rows), jnp.bfloat16),
            pltpu.VMEM((lines, 2 * rows, rows), jnp.bfloat16),
            pltpu.SemaphoreType.DMA((2 + 4 * len(shifts) + lines,)),
        ],
        compiler_params=limit,
        cost_estimate=small,
        name="weights",
    )(block_owner, rows_live, coefficients, pltpu.with_memory_space_constraint(y_operator, HBM))

    tiles = x_length // TILE
    def own_terms(w_own):
        return pl.pallas_call(
            own_kernel,
            grid=(tiles,),
            in_specs=[smem()] * 3
            + [
                pl.BlockSpec(w_own.shape, lambda n: (0, 0)),
                pl.BlockSpec((1, nvar, rows, x_length), lambda n: (0, 0, 0, 0)),
                pl.BlockSpec((1, nvar, rows, TILE), lambda n: (0, 0, 0, n)),
                pl.BlockSpec((x_length, TILE), lambda n: (0, n)),
                pl.BlockSpec((x_length, TILE), lambda n: (0, n + tiles)),
            ],
            out_specs=pl.BlockSpec((1, nvar, rows, TILE), lambda n: (0, 0, 0, n)),
            out_shape=state_shape,
            scratch_shapes=[
                pltpu.VMEM((nvar * rows, x_length), jnp.bfloat16),
                pltpu.VMEM((nvar * rows, x_length), jnp.bfloat16),
            ],
            compiler_params=limit,
            cost_estimate=small,
            name="own_terms",
        )(
            block_owner,
            rows_live,
            coefficients,
            w_own,
            flow_state,
            flow_state,
            *[pltpu.with_memory_space_constraint(x_operator, HBM)] * 2,
        )

    far_v = [direct_first[shifts.index(lines - s)] for s in shifts]
    sent = jax.ShapeDtypeStruct((1, len(SENT), rows, x_length), jnp.float32)
    send = pl.pallas_call(
        send_kernel,
        in_specs=[kept()] * (3 + len(SENT) + len(shifts)),
        out_specs=[kept()] * len(shifts),
        out_shape=[sent] * len(shifts),
        compiler_params=limit,
        cost_estimate=small,
        name="send_terms",
    )
    arrived = [faces]
    held_faces, step = faces, 1
    while step < slots:
        there = lax.ppermute(held_faces, "blk", [(i, i ^ step) for i in range(slots)])
        if step == 1:
            there, w_own, own = lax.optimization_barrier((there, w_own, flow_state))
            near_v = lax.ppermute(own[:, 1:2], "line", sibling)
        elif step == 2:
            w_send, *_ = lax.optimization_barrier((w_send, there))
            results = send(*map(held, (w_send, nu, flow_state, *far_v, *near)))
            direct_first, *_ = lax.optimization_barrier((direct_first, *results))
            direct_second, *_ = lax.optimization_barrier((direct_second, *results))
            w_own, *_ = lax.optimization_barrier((w_own, *results))
            state = own_terms(w_own)
        arrived.append(there)
        step *= 2
        if step < slots:
            held_faces = jnp.concatenate([held_faces, there], axis=0)

    results = [
        lax.ppermute(result, "line", [(i, (i + s) % lines) for i in range(lines)])
        for s, result in zip(shifts, results)
    ]

    def sibling_terms(part, direct):
        operands = [*map(held, (w_sibling, nu, flow_state, near_v, *direct))]
        low, high = part
        results = pl.pallas_call(
            functools.partial(sibling_kernel, low, high),
            in_specs=[kept()] * len(operands),
            out_specs=[kept()] * (high - low),
            out_shape=[jax.ShapeDtypeStruct((1, 1, rows, x_length), jnp.float32)] * (high - low),
            compiler_params=limit,
            cost_estimate=small,
            name="sibling_terms",
        )(*operands)
        return [*direct, *(lax.ppermute(result, "line", sibling) for result in results)]

    direct_second, *_ = lax.optimization_barrier((direct_second, *arrived))
    pieces = sibling_terms(FIRST, direct_first) + sibling_terms(SECOND, direct_second)

    anywhere = pl.BlockSpec(memory_space=pl.ANY)
    result, left = pl.pallas_call(
        functools.partial(near_kernel, len(arrived)),
        in_specs=[smem()] * 4 + [kept()] * (6 + len(SENT) + len(arrived) + len(pieces)),
        out_specs=[anywhere, kept()],
        out_shape=[state_shape, sent],
        scratch_shapes=[
            pltpu.VMEM((len(RAW), rows, x_length), jnp.float32),
            pltpu.SemaphoreType.DMA((len(RAW),)),
        ],
        compiler_params=limit,
        cost_estimate=small,
        name="near_terms",
    )(
        block_owner,
        link_block.T,
        link_side.T,
        rows_live,
        *map(held, (ghost_operator, w_near, w_direct, nu, flow_state, state, *near, *arrived, *pieces)),
    )

    operands = [*map(held, (left, *results))]
    return pl.pallas_call(
        last_kernel,
        in_specs=[kept()] * len(operands) + [anywhere],
        out_specs=anywhere,
        out_shape=state_shape,
        input_output_aliases={len(operands): 0},
        scratch_shapes=[pltpu.VMEM(sent.shape[1:], jnp.float32), pltpu.SemaphoreType.DMA((len(SENT),))],
        compiler_params=limit,
        cost_estimate=small,
        name="last_terms",
    )(*operands, result)


def solution(mesh):
    return jax.shard_map(
        functools.partial(on_device, mesh.shape["blk"], mesh.shape["line"]),
        mesh=mesh,
        in_specs=(P("blk", None, "line", None), P(), P(), P(), P(), P(), P(), P(), P()),
        out_specs=P("blk", None, "line", None),
        check_vma=False,
    )
```
